32 devices in a mesh: row: 4 (over x, core), col: 8 (over z, y).
Axes of the slice: x: 2, y: 2, z: 4, core: 2. Of those that a mesh axis runs over, the one named last changes fastest.
Arguments:
- strain: bfloat16 [32, 192000], P(('row', 'col')), may hold values from -500 to 500
- seg_offsets: int32 [32], replicated, may hold values from 0 to 186000, as said below
- band_bins: int32 [512], replicated, may hold values from 60 to 1083, as said below
Outputs:
- stacked: float32 [32, 4, 8, 2, 512], P('row', None, 'col')
The draws below stay inside these ranges and needn't reach their ends.
Inputs may be any that keep to these rules, and one draw needn't show every extreme that they name: `seg_offsets`: segment 0 starts the record and the last segment ends it; each other segment s starts between s * 6000 - 6000 // 2 and s * 6000. `band_bins`: strictly increasing.
All inputs are finite; a program needn't handle non-finite values.
Results may differ from the reference program's by a relative error of at most 0.0064.
Values may be sent and summed in bfloat16 or wider, within the bound.
No kernel may reach another device: no remote copies, remote signals or barrier semaphores. Data moves between devices by JAX's collectives and lax.ppermute only.
A program may use at most 192 MiB of HBM per device.

```python
import math
import jax
import jax.numpy as jnp
from jax import lax

F = 512
SEGLEN = 6000
SEG = 32
NSUB = 5
TAPER = 32
SMOOTH = 64
B_LO = 60
CH = 32
REC = 192000
N_ROW = 4
N_COL = 8


def draw_strain(key, part):
    keys = jax.random.split(jax.random.fold_in(key, 11), 4)
    blocks = REC // SEGLEN
    position = jnp.arange(CH, dtype=jnp.float32) / max(CH - 1, 1)
    level = jnp.exp(jax.random.uniform(keys[0], (blocks,), jnp.float32, 0.0, math.log(4.0)))
    direction = (jax.random.randint(keys[1], (blocks,), 0, 2) * 2 - 1).astype(jnp.float32)
    spread = jnp.exp(jax.random.uniform(keys[2], (CH, blocks), jnp.float32, 0.0, math.log(10.0)))
    base = 3.0
    noise = jnp.clip(jax.random.normal(keys[3], (CH, REC), jnp.float32), -6.0, 6.0)
    profile = jnp.power(base, direction[None, :] * (position[:, None] - 0.5))
    amplitude = level[None, :] * spread * profile
    amplitude = jnp.repeat(amplitude, SEGLEN, axis=1)
    return (noise * amplitude).astype(jnp.bfloat16)


def draw_seg_offsets(key, part):
    jitter = jax.random.randint(jax.random.fold_in(key, 23), (SEG,), 0, SEGLEN // 2 + 1)
    index = jnp.arange(SEG, dtype=jnp.int32)
    nominal = index * SEGLEN
    middle = nominal - jitter
    return jnp.where(index == 0, 0, jnp.where(index == SEG - 1, nominal, middle)).astype(jnp.int32)


def draw_band_bins(key, part):
    jitter = jax.random.randint(jax.random.fold_in(key, 37), (F,), 0, 2)
    index = jnp.arange(F, dtype=jnp.int32)
    jitter = jnp.where(index == 0, 0, jnp.where(index == F - 1, 1, jitter))
    return (B_LO + 2 * index + jitter).astype(jnp.int32)


def setup_inputs(seed: int = 0) -> dict:
    splits = jax.random.split(jax.random.key(seed), 4)
    strain = draw_strain(jax.random.fold_in(splits[3], 71), 0)
    seg_offsets = draw_seg_offsets(jax.random.fold_in(splits[3], 71), 0)
    band_bins = draw_band_bins(jax.random.fold_in(splits[3], 71), 0)
    return dict(strain=strain, seg_offsets=seg_offsets, band_bins=band_bins)


def build_tables(band_bins):
    inner_len = SEGLEN // NSUB
    inner = jnp.arange(inner_len, dtype=jnp.int32)
    phase = inner[:, None] * band_bins[None, :] % SEGLEN
    angle = phase.astype(jnp.float32) * (2.0 * math.pi / SEGLEN)
    table = jnp.concatenate([jnp.cos(angle), -jnp.sin(angle)], axis=1).astype(jnp.bfloat16)
    outer = jnp.arange(NSUB, dtype=jnp.int32)
    outer_phase = outer[:, None] * (band_bins[None, :] * inner_len) % SEGLEN
    outer_angle = outer_phase.astype(jnp.float32) * (2.0 * math.pi / SEGLEN)
    twist_re = jnp.cos(outer_angle)
    twist_im = -jnp.sin(outer_angle)
    samples = jnp.arange(SEGLEN, dtype=jnp.float32)
    window = 0.5 - 0.5 * jnp.cos(samples * (2.0 * math.pi / SEGLEN))
    freq = jnp.arange(F, dtype=jnp.float32) + 0.5
    reach = jnp.minimum(jnp.minimum(freq, F - freq) / TAPER, 1.0)
    band_taper = jnp.square(jnp.sin(0.5 * math.pi * reach))
    lower = jnp.clip(jnp.arange(F, dtype=jnp.int32) - SMOOTH // 2, 0, F - SMOOTH)
    source = jnp.arange(F, dtype=jnp.int32)
    inside = (source[:, None] >= lower[None, :]) & (source[:, None] < lower[None, :] + SMOOTH)
    average = inside.astype(jnp.float32) / SMOOTH
    return (table, twist_re, twist_im, window, band_taper, average)

def taper_segments(records, seg_offsets, window):

    def one_segment(begin):
        return lax.dynamic_slice_in_dim(records, begin, SEGLEN, 1)
    segments = jax.vmap(one_segment)(seg_offsets)
    return (segments.astype(jnp.float32) * window).astype(jnp.bfloat16)

def spectra_of(tapered, tables):
    table, twist_re, twist_im, window, band_taper, average = tables
    count = tapered.shape[1]
    inner_len = SEGLEN // NSUB
    total_rows = SEG * count
    flattened = tapered.reshape(total_rows, NSUB, inner_len)
    spec_re = jnp.zeros((total_rows, F), jnp.float32)
    spec_im = jnp.zeros((total_rows, F), jnp.float32)
    for block in range(NSUB):
        part = jnp.dot(flattened[:, block, :], table, preferred_element_type=jnp.float32)
        part_re = part[:, :F]
        part_im = part[:, F:]
        spec_re = spec_re + part_re * twist_re[block] - part_im * twist_im[block]
        spec_im = spec_im + part_re * twist_im[block] + part_im * twist_re[block]
    power = spec_re * spec_re + spec_im * spec_im
    smooth = jnp.dot(power, average, precision=lax.Precision.HIGHEST)
    scale = band_taper * lax.rsqrt(smooth + 1e-06)
    whitened = jnp.concatenate([spec_re * scale, spec_im * scale], axis=1).astype(jnp.bfloat16)
    return whitened.reshape(SEG, count, 2 * F)

def segment_share(energy, channels):
    weights = 1.0 / (energy / (channels * SEGLEN) + 1e-06)
    return weights / jnp.sum(weights)

def cross_spectra(row_side, col_side, share):
    left = row_side.astype(jnp.float32) * share[:, None, None]
    right = col_side.astype(jnp.float32)
    left_re, left_im = (left[..., :F], left[..., F:])
    right_re, right_im = (right[..., :F], right[..., F:])
    high = lax.Precision.HIGHEST
    real = jnp.einsum('sif,sjf->ijf', left_re, right_re, precision=high) + jnp.einsum('sif,sjf->ijf', left_im, right_im, precision=high)
    imag = jnp.einsum('sif,sjf->ijf', left_im, right_re, precision=high) - jnp.einsum('sif,sjf->ijf', left_re, right_im, precision=high)
    return jnp.stack([real, imag], axis=2)

def reference(strain, seg_offsets, band_bins):
    tables = build_tables(band_bins)
    tapered = taper_segments(strain, seg_offsets, tables[3])
    energy = lax.optimization_barrier(jnp.sum(jnp.square(tapered.astype(jnp.float32)), axis=(1, 2)))
    share = segment_share(energy, CH)
    spectra = spectra_of(tapered, tables)
    row_blocks = spectra.reshape(SEG, N_ROW, N_COL, 2 * F).transpose(1, 0, 2, 3)

    def one_block(block_spectra):
        return cross_spectra(block_spectra, spectra, share)
    result = lax.map(one_block, row_blocks)
    return result.reshape(CH, N_ROW, N_COL, 2, F)
```

```python
import functools
import math

import jax
import jax.numpy as jnp
import numpy as np
from jax import lax
from jax.experimental import pallas as pl
from jax.experimental.pallas import tpu as pltpu
from jax.sharding import PartitionSpec as P

SEGLEN = 6000
TAPER = 32
SMOOTH = 64
EPS = 1e-06
LANES = 128
DEPTH = 256
EDGE = 16


def window_constants(rows):
    position = np.arange(rows * DEPTH, dtype=np.float64).reshape(rows, DEPTH)
    angle = 2.0 * math.pi / SEGLEN * position
    both = np.concatenate([0.5 * np.cos(angle), 0.5 * np.sin(angle)], axis=0)
    return both.astype(np.float32)


def ramp_constant(width):
    freq = np.arange(width, dtype=np.float64) + 0.5
    reach = np.minimum(np.minimum(freq, width - freq) / TAPER, 1.0)
    return np.square(np.sin(0.5 * math.pi * reach)).astype(np.float32)[None, :]


def transform_kernel(
    count, rows, width, offsets, strain, bins, trig, ramp, spectra, energy,
    record, shift, tapered, parts, table, waves,
):
    samples = strain.shape[1]
    chunk = LANES * 8 * 8
    begin = 0
    while begin < samples:
        size = min(chunk, samples - begin)
        part = strain[:, begin : begin + size].astype(jnp.float32)
        record[begin // LANES : (begin + size) // LANES, :] = part.reshape(size // LANES, LANES)
        begin += size
    tail = record.shape[0] - samples // LANES
    record[samples // LANES :, :] = jnp.zeros((tail, LANES), jnp.float32)

    mult_row = lax.broadcasted_iota(jnp.int32, (2 * EDGE + rows, 1), 0)
    mult = jnp.where(
        mult_row < EDGE,
        mult_row,
        jnp.where(mult_row < 2 * EDGE, (mult_row - EDGE) * EDGE, (mult_row - 2 * EDGE) * DEPTH),
    ).astype(jnp.float32)
    phase = mult * bins[...].reshape(1, width).astype(jnp.float32)
    turns = jnp.floor(phase * (1.0 / SEGLEN) + 0.5)
    angle = (phase - turns * SEGLEN) * (2.0 * math.pi / SEGLEN)
    waves[0] = jnp.cos(angle)
    waves[1] = jnp.sin(angle)
    tiles = width // LANES
    low_cos = waves[0, 0:EDGE, :]
    low_sin = waves[1, 0:EDGE, :]
    for high in range(DEPTH // EDGE):
        at = EDGE + high
        high_cos = waves[0, at : at + 1, :]
        high_sin = waves[1, at : at + 1, :]
        real = high_cos * low_cos - high_sin * low_sin
        imag = -(high_sin * low_cos + high_cos * low_sin)
        for tile in range(tiles):
            cut = slice(tile * LANES, (tile + 1) * LANES)
            to = 2 * tile * LANES
            here = slice(high * EDGE, (high + 1) * EDGE)
            table[here, to : to + LANES] = real[:, cut].astype(jnp.bfloat16)
            table[here, to + LANES : to + 2 * LANES] = imag[:, cut].astype(jnp.bfloat16)

    for s in range(count):
        inside = (offsets[s] & (LANES - 1)).astype(jnp.float32)
        shift[0, s : s + 1, :] = jnp.full((1, LANES), inside, jnp.float32)
    turn = shift[0] * (2.0 * math.pi / SEGLEN)
    shift[1] = jnp.cos(turn)
    shift[2] = jnp.sin(turn)
    place = (
        lax.broadcasted_iota(jnp.int32, (8, LANES), 0) * DEPTH
        + lax.broadcasted_iota(jnp.int32, (8, LANES), 1)
    ).astype(jnp.float32)
    for s in range(count):
        first = offsets[s] // LANES
        moved = place - shift[0, s : s + 1, :]
        turn_cos = shift[1, s : s + 1, :]
        turn_sin = shift[2, s : s + 1, :]
        total = jnp.zeros((8, LANES), jnp.float32)
        for group in range(rows // 8):
            for half in range(DEPTH // LANES):
                block = record[pl.ds(first + half + 16 * group, 8, stride=2), :]
                lanes = slice(half * LANES, (half + 1) * LANES)
                wave_cos = trig[group * 8 : group * 8 + 8, lanes]
                wave_sin = trig[rows + group * 8 : rows + group * 8 + 8, lanes]
                window = 0.5 - (wave_cos * turn_cos + wave_sin * turn_sin)
                value = block * window
                sample = group * 8 * DEPTH + half * LANES
                if group == 0 and half == 0:
                    value = jnp.where(moved > -0.5, value, 0.0)
                if (group + 1) * 8 * DEPTH > SEGLEN - DEPTH:
                    value = jnp.where(moved < SEGLEN - sample - 0.5, value, 0.0)
                value = value.astype(jnp.bfloat16).astype(jnp.float32)
                total = total + value * value
                tapered[half, pl.ds(s + group * 8 * count, 8, stride=count), :] = value
        energy[s : s + 1, :] = jnp.sum(total, axis=0, keepdims=True)

    left = jnp.concatenate(
        [tapered[half].astype(jnp.bfloat16) for half in range(DEPTH // LANES)], axis=1
    )
    for tile in range(tiles):
        cut = slice(tile * LANES, (tile + 1) * LANES)
        to = 2 * tile * LANES
        product = jnp.dot(left, table[:, to : to + 2 * LANES], preferred_element_type=jnp.float32)
        real = jnp.zeros((count, LANES), jnp.float32)
        imag = jnp.zeros((count, LANES), jnp.float32)
        for r in range(rows):
            part = product[r * count : (r + 1) * count, :]
            twist_re = waves[0, 2 * EDGE + r : 2 * EDGE + r + 1, cut]
            twist_im = -waves[1, 2 * EDGE + r : 2 * EDGE + r + 1, cut]
            part_re, part_im = part[:, :LANES], part[:, LANES:]
            real = real + (part_re * twist_re - part_im * twist_im)
            imag = imag + (part_re * twist_im + part_im * twist_re)
        parts[0, :, cut] = real
        parts[1, :, cut] = imag
    real, imag = parts[0], parts[1]
    summed = real * real + imag * imag
    reach = 1
    while reach < SMOOTH:
        summed = summed + pltpu.roll(summed, width - reach, 1)
        reach *= 2
    lane = lax.broadcasted_iota(jnp.int32, (count, width), 1)
    middle = pltpu.roll(summed, SMOOTH // 2, 1)
    middle = jnp.where(lane < SMOOTH // 2, summed[:, 0:1], middle)
    last = width - SMOOTH
    middle = jnp.where(lane >= last + SMOOTH // 2, summed[:, last : last + 1], middle)
    scale = ramp[...] * lax.rsqrt(middle * (1.0 / SMOOTH) + EPS)
    spectra[:, 0:width] = (real * scale).astype(jnp.bfloat16)
    spectra[:, width:] = (imag * scale).astype(jnp.bfloat16)


def transform(strain, offsets, bins):
    count, width = offsets.shape[0], bins.shape[0]
    samples = strain.shape[1]
    rows = -(-(SEGLEN + LANES - 1) // DEPTH)
    lines = -(-(samples // LANES + 2) // 8) * 8
    vmem = pl.BlockSpec(memory_space=pltpu.VMEM)
    return pl.pallas_call(
        functools.partial(transform_kernel, count, rows, width),
        out_shape=[
            jax.ShapeDtypeStruct((count, 2 * width), jnp.bfloat16),
            jax.ShapeDtypeStruct((count, LANES), jnp.float32),
        ],
        in_specs=[pl.BlockSpec(memory_space=pltpu.SMEM)] + [vmem] * 4,
        out_specs=[vmem, vmem],
        scratch_shapes=[
            pltpu.VMEM((lines, LANES), jnp.float32),
            pltpu.VMEM((3, count, LANES), jnp.float32),
            pltpu.VMEM((DEPTH // LANES, rows * count, LANES), jnp.float32),
            pltpu.VMEM((2, count, width), jnp.float32),
            pltpu.VMEM((DEPTH, 2 * width), jnp.bfloat16),
            pltpu.VMEM((2, 2 * EDGE + rows, width), jnp.float32),
        ],
        compiler_params=pltpu.CompilerParams(vmem_limit_bytes=40 << 20),
        name="transform",
    )(offsets, strain, bins, window_constants(rows), ramp_constant(width))


def cross_kernel(left_count, right_count, places, share, *refs):
    left, right = refs[:left_count], refs[left_count : left_count + right_count]
    out = refs[-1]
    count = share.shape[0]
    width = left[0].shape[1] // 2
    for tile in range(width // LANES):
        cut = slice(tile * LANES, (tile + 1) * LANES)
        cut_im = slice(width + tile * LANES, width + (tile + 1) * LANES)
        rights = [
            (ref[:, cut].astype(jnp.float32), ref[:, cut_im].astype(jnp.float32)) for ref in right
        ]
        for i, ref in enumerate(left):
            left_re = ref[:, cut].astype(jnp.float32) * share[...]
            left_im = ref[:, cut_im].astype(jnp.float32) * share[...]
            for j, (right_re, right_im) in enumerate(rights):
                real = left_re * right_re + left_im * right_im
                imag = left_im * right_re - left_re * right_im
                at = places[i], places[left_count + j]
                out[at[0], at[1], 0, 0:1, cut] = jnp.sum(real, axis=0, keepdims=True)
                out[at[0], at[1], 0, 1:2, cut] = jnp.sum(imag, axis=0, keepdims=True)


def cross(places, share, left, right):
    width = left[0].shape[1] // 2
    vmem = pl.BlockSpec(memory_space=pltpu.VMEM)
    return pl.pallas_call(
        functools.partial(cross_kernel, len(left), len(right)),
        out_shape=jax.ShapeDtypeStruct((len(left), len(right), 1, 2, width), jnp.float32),
        in_specs=[pl.BlockSpec(memory_space=pltpu.SMEM)] + [vmem] * (1 + len(left) + len(right)),
        out_specs=vmem,
        compiler_params=pltpu.CompilerParams(vmem_limit_bytes=40 << 20),
        name="cross",
    )(places, share, *left, *right)


def partners(size):
    if size & (size - 1) == 0:
        return [lambda p, k=k: p ^ k for k in range(size)]
    return [lambda p, k=k: (p - k) % size for k in range(size)]


def exchange(x, axis, size):
    out = []
    for source in partners(size)[1:]:
        pairs = [(source(p), p) for p in range(size)]
        out.append(lax.ppermute(x, axis, pairs))
    return out


def per_device(strain, offsets, bins):
    row_size, col_size = lax.axis_size("row"), lax.axis_size("col")
    spectra, partial = transform(strain, offsets, bins)
    own = jnp.sum(partial, axis=1)
    energy = lax.psum(own, ("row", "col"))
    weight = 1.0 / (energy / (row_size * col_size * SEGLEN) + EPS)
    share = weight / jnp.sum(weight)
    share = jnp.broadcast_to(share[:, None], (share.shape[0], LANES))
    row, col = lax.axis_index("row"), lax.axis_index("col")
    left = [spectra] + exchange(spectra, "col", col_size)
    right = [spectra] + exchange(spectra, "row", row_size)
    places = jnp.stack(
        [f(col) for f in partners(col_size)] + [f(row) for f in partners(row_size)]
    ).astype(jnp.int32)
    return cross(places, share, left, right)


def solution(mesh):
    placed = (P(("row", "col"), None), P(), P())
    return jax.shard_map(
        per_device,
        mesh=mesh,
        in_specs=placed,
        out_specs=P("row", None, "col", None, None),
        check_vma=False,
    )
```

```python
import functools
import math

import jax
import jax.numpy as jnp
import numpy as np
from jax import lax
from jax.experimental import pallas as pl
from jax.experimental.pallas import tpu as pltpu
from jax.sharding import Mesh
from jax.sharding import PartitionSpec as P

SEGLEN = 6000
TAPER = 32
SMOOTH = 64
EPS = 1e-06
LANES = 128
DEPTH = 256
VMEM_LIMIT = 58 << 20
CROSS_VMEM = 16 << 20
EXTRA = 16
PIECES = 3
EDGE = 16


def window_constants(rows):
    position = np.arange(rows * DEPTH, dtype=np.float64).reshape(rows, DEPTH)
    angle = 2.0 * math.pi / SEGLEN * position
    both = np.concatenate([0.5 * np.cos(angle), 0.5 * np.sin(angle)], axis=0)
    return both.astype(np.float32)


def ramp_constant(width):
    freq = np.arange(width, dtype=np.float64) + 0.5
    reach = np.minimum(np.minimum(freq, width - freq) / TAPER, 1.0)
    return np.square(np.sin(0.5 * math.pi * reach)).astype(np.float32)[None, :]


def transform_kernel(
    count, rows, width, offsets_hbm, strain_hbm, bins_hbm, trig_hbm, ramp_hbm, payload,
    offsets, strain, bins, trig, ramp, record, shift, blocks, sums, parts, table, waves, sems,
):
    arrivals = [
        pltpu.make_async_copy(source, target, sems.at[i])
        for i, (source, target) in enumerate(
            [
                (bins_hbm, bins),
                (offsets_hbm, offsets),
                (strain_hbm, strain),
                (trig_hbm, trig),
                (ramp_hbm, ramp),
            ]
        )
    ]
    for copy in arrivals:
        copy.start()

    arrivals[0].wait()
    mult_row = lax.broadcasted_iota(jnp.int32, (2 * EDGE + rows, 1), 0)
    mult = jnp.where(
        mult_row < EDGE,
        mult_row,
        jnp.where(mult_row < 2 * EDGE, (mult_row - EDGE) * EDGE, (mult_row - 2 * EDGE) * DEPTH),
    ).astype(jnp.float32)
    phase = mult * bins[...].reshape(1, width).astype(jnp.float32)
    turns = jnp.floor(phase * (1.0 / SEGLEN) + 0.5)
    angle = (phase - turns * SEGLEN) * (2.0 * math.pi / SEGLEN)
    waves[0] = jnp.cos(angle)
    waves[1] = jnp.sin(angle)
    tiles = width // LANES
    low_cos = waves[0, 0:EDGE, :]
    low_sin = waves[1, 0:EDGE, :]
    for high in range(DEPTH // EDGE):
        at = EDGE + high
        high_cos = waves[0, at : at + 1, :]
        high_sin = waves[1, at : at + 1, :]
        real = high_cos * low_cos - high_sin * low_sin
        imag = -(high_sin * low_cos + high_cos * low_sin)
        for tile in range(tiles):
            cut = slice(tile * LANES, (tile + 1) * LANES)
            to = 2 * tile * LANES
            here = slice(high * EDGE, (high + 1) * EDGE)
            table[here, to : to + LANES] = real[:, cut].astype(jnp.bfloat16)
            table[here, to + LANES : to + 2 * LANES] = imag[:, cut].astype(jnp.bfloat16)
    arrivals[1].wait()
    for s in range(count):
        inside = (offsets[s] & (LANES - 1)).astype(jnp.float32)
        shift[0, s : s + 1, :] = jnp.full((1, LANES), inside, jnp.float32)
    turn = shift[0] * (2.0 * math.pi / SEGLEN)
    shift[1] = jnp.cos(turn)
    shift[2] = jnp.sin(turn)
    for copy in arrivals[2:]:
        copy.wait()
    samples = strain.shape[1]
    chunk = LANES * 8 * 8
    begin = 0
    while begin < samples:
        size = min(chunk, samples - begin)
        part = strain[:, begin : begin + size].astype(jnp.float32)
        record[begin // LANES : (begin + size) // LANES, :] = part.reshape(size // LANES, LANES)
        begin += size
    tail = record.shape[0] - samples // LANES
    record[samples // LANES :, :] = jnp.zeros((tail, LANES), jnp.float32)
    place = (
        lax.broadcasted_iota(jnp.int32, (8, LANES), 0) * DEPTH
        + lax.broadcasted_iota(jnp.int32, (8, LANES), 1)
    ).astype(jnp.float32)
    for s in range(count):
        first = offsets[s] // LANES
        moved = place - shift[0, s : s + 1, :]
        turn_cos = shift[1, s : s + 1, :]
        turn_sin = shift[2, s : s + 1, :]
        total = jnp.zeros((8, LANES), jnp.float32)
        for group in range(rows // 8):
            for half in range(DEPTH // LANES):
                block = record[pl.ds(first + half + 16 * group, 8, stride=2), :]
                lanes = slice(half * LANES, (half + 1) * LANES)
                wave_cos = trig[group * 8 : group * 8 + 8, lanes]
                wave_sin = trig[rows + group * 8 : rows + group * 8 + 8, lanes]
                window = 0.5 - (wave_cos * turn_cos + wave_sin * turn_sin)
                value = block * window
                sample = group * 8 * DEPTH + half * LANES
                if group == 0 and half == 0:
                    value = jnp.where(moved > -0.5, value, 0.0)
                if (group + 1) * 8 * DEPTH > SEGLEN - DEPTH:
                    value = jnp.where(moved < SEGLEN - sample - 0.5, value, 0.0)
                value = value.astype(jnp.bfloat16).astype(jnp.float32)
                total = total + value * value
                blocks[half, pl.ds(s + group * 8 * count, 8, stride=count), :] = value
        sums[s : s + 1, :] = jnp.sum(total, axis=0, keepdims=True)
    tapered = jnp.concatenate(
        [blocks[half].astype(jnp.bfloat16) for half in range(DEPTH // LANES)], axis=1
    )
    lane = lax.broadcasted_iota(jnp.int32, (count, LANES), 1)
    line = lax.broadcasted_iota(jnp.int32, (count, LANES), 0)
    whole = jnp.sum(sums[...], axis=1, keepdims=True)
    rest = jnp.sum(jnp.where(lane == line, whole, 0.0), axis=0, keepdims=True)
    place = lax.broadcasted_iota(jnp.int32, (EXTRA, LANES), 0)
    extra = jnp.zeros((EXTRA, LANES), jnp.float32)
    for i in range(PIECES):
        piece = rest.astype(jnp.bfloat16).astype(jnp.float32)
        extra = jnp.where(place == i, piece, extra)
        rest = rest - piece
    payload[2 * tiles * count :, :] = extra.astype(jnp.bfloat16)

    for tile in range(tiles):
        cut = slice(tile * LANES, (tile + 1) * LANES)
        to = 2 * tile * LANES
        product = jnp.dot(
            tapered, table[:, to : to + 2 * LANES], preferred_element_type=jnp.float32
        )
        real = jnp.zeros((count, LANES), jnp.float32)
        imag = jnp.zeros((count, LANES), jnp.float32)
        for r in range(rows):
            part = product[r * count : (r + 1) * count, :]
            twist_re = waves[0, 2 * EDGE + r : 2 * EDGE + r + 1, cut]
            twist_im = -waves[1, 2 * EDGE + r : 2 * EDGE + r + 1, cut]
            part_re, part_im = part[:, :LANES], part[:, LANES:]
            real = real + (part_re * twist_re - part_im * twist_im)
            imag = imag + (part_re * twist_im + part_im * twist_re)
        parts[0, :, cut] = real
        parts[1, :, cut] = imag
    real, imag = parts[0], parts[1]
    summed = real * real + imag * imag
    reach = 1
    while reach < SMOOTH:
        summed = summed + pltpu.roll(summed, width - reach, 1)
        reach *= 2
    lane = lax.broadcasted_iota(jnp.int32, (count, width), 1)
    middle = pltpu.roll(summed, SMOOTH // 2, 1)
    middle = jnp.where(lane < SMOOTH // 2, summed[:, 0:1], middle)
    last = width - SMOOTH
    middle = jnp.where(lane >= last + SMOOTH // 2, summed[:, last : last + 1], middle)
    scale = ramp[...] * lax.rsqrt(middle * (1.0 / SMOOTH) + EPS)
    real, imag = (real * scale).astype(jnp.bfloat16), (imag * scale).astype(jnp.bfloat16)
    for tile in range(tiles):
        cut = slice(tile * LANES, (tile + 1) * LANES)
        payload[2 * tile * count : (2 * tile + 1) * count, :] = real[:, cut]
        payload[(2 * tile + 1) * count : (2 * tile + 2) * count, :] = imag[:, cut]


def transform(strain, offsets, bins):
    count, width = offsets.shape[0], bins.shape[0]
    samples = strain.shape[1]
    rows = -(-(SEGLEN + LANES - 1) // DEPTH)
    lines = -(-(samples // LANES + 2) // 8) * 8
    trig, ramp = window_constants(rows), ramp_constant(width)
    vmem = pl.BlockSpec(memory_space=pltpu.VMEM)
    hbm = pl.BlockSpec(memory_space=pltpu.HBM)
    return pl.pallas_call(
        functools.partial(transform_kernel, count, rows, width),
        out_shape=jax.ShapeDtypeStruct((2 * width // LANES * count + EXTRA, LANES), jnp.bfloat16),
        in_specs=[hbm] * 5,
        out_specs=vmem,
        scratch_shapes=[
            pltpu.SMEM(offsets.shape, jnp.int32),
            pltpu.VMEM(strain.shape, strain.dtype),
            pltpu.VMEM(bins.shape, jnp.int32),
            pltpu.VMEM(trig.shape, jnp.float32),
            pltpu.VMEM(ramp.shape, jnp.float32),
            pltpu.VMEM((lines, LANES), jnp.float32),
            pltpu.VMEM((3, count, LANES), jnp.float32),
            pltpu.VMEM((DEPTH // LANES, rows * count, LANES), jnp.float32),
            pltpu.VMEM((count, LANES), jnp.float32),
            pltpu.VMEM((2, count, width), jnp.float32),
            pltpu.VMEM((DEPTH, 2 * width), jnp.bfloat16),
            pltpu.VMEM((2, 2 * EDGE + rows, width), jnp.float32),
            pltpu.SemaphoreType.DMA((5,)),
        ],
        compiler_params=pltpu.CompilerParams(vmem_limit_bytes=VMEM_LIMIT),
        cost_estimate=pl.CostEstimate(flops=400 << 20, bytes_accessed=6 << 20, transcendentals=0),
        name="transform",
    )(offsets, strain, bins, trig, ramp)


def energy_of(payload):
    return jnp.sum(payload[-EXTRA:, :].astype(jnp.float32), axis=0, keepdims=True)


def share_of(energy, count, channels):
    lane = lax.broadcasted_iota(jnp.int32, (count, LANES), 1)
    line = lax.broadcasted_iota(jnp.int32, (count, LANES), 0)
    weight = 1.0 / (energy * (1.0 / (channels * SEGLEN)) + EPS)
    weight = jnp.where(lane[0:1] < count, weight, 0.0)
    weight = weight / jnp.sum(weight, axis=1, keepdims=True)
    column = jnp.sum(jnp.where(lane == line, weight, 0.0), axis=1, keepdims=True)
    return jnp.broadcast_to(column, (count, LANES))


def cross_kernel(left_count, right_count, count, channels, places, energy, *refs):
    left, right = refs[:left_count], refs[left_count : left_count + right_count]
    out, block, sems = refs[left_count + right_count :]
    share = share_of(energy[...], count, channels)
    tiles = block.shape[-1] // LANES
    copies = [
        pltpu.make_async_copy(block.at[i], out.at[places[right_count + i]], sems.at[i])
        for i in range(left_count)
    ]
    for i, ref in enumerate(left):
        for tile in range(tiles):
            cut = slice(tile * LANES, (tile + 1) * LANES)
            at_re = slice(2 * tile * count, (2 * tile + 1) * count)
            at_im = slice((2 * tile + 1) * count, (2 * tile + 2) * count)
            left_re = ref[at_re, :].astype(jnp.float32) * share
            left_im = ref[at_im, :].astype(jnp.float32) * share
            for j, other in enumerate(right):
                right_re = other[at_re, :].astype(jnp.float32)
                right_im = other[at_im, :].astype(jnp.float32)
                real = left_re * right_re + left_im * right_im
                imag = left_im * right_re - left_re * right_im
                at = places[j]
                block[i, at, 0, 0:1, cut] = jnp.sum(real, axis=0, keepdims=True)
                block[i, at, 0, 1:2, cut] = jnp.sum(imag, axis=0, keepdims=True)
        copies[i].start()
    for copy in copies:
        copy.wait()


def cross(places, energy, left, right, count, width, channels):
    vmem = pl.BlockSpec(memory_space=pltpu.VMEM)
    arrays = [energy, *left, *right]
    return pl.pallas_call(
        functools.partial(cross_kernel, len(left), len(right), count, channels),
        out_shape=jax.ShapeDtypeStruct((len(left), len(right), 1, 2, width), jnp.float32),
        in_specs=[pl.BlockSpec(memory_space=pltpu.SMEM)] + [vmem] * len(arrays),
        out_specs=pl.BlockSpec(memory_space=pltpu.HBM),
        scratch_shapes=[
            pltpu.VMEM((len(left), len(right), 1, 2, width), jnp.float32),
            pltpu.SemaphoreType.DMA((len(left),)),
        ],
        compiler_params=pltpu.CompilerParams(vmem_limit_bytes=CROSS_VMEM),
        cost_estimate=pl.CostEstimate(flops=4 << 20, bytes_accessed=2 << 20, transcendentals=0),
        name="cross",
    )(places, *arrays)


def partners(size):
    if size & (size - 1) == 0:
        return [lambda p, k=k: p ^ k for k in range(size)]
    return [lambda p, k=k: (p - k) % size for k in range(size)]


def fetch(x, axis, size, step):
    source = partners(size)[step]
    return lax.ppermute(x, axis, [(source(p), p) for p in range(size)])


def fetch_all(x, axis, size):
    return [fetch(x, axis, size, step) for step in range(size - 1, 0, -1)][::-1]


def per_device(row_size, col_size, strain, offsets, bins):
    axes = ("x", "c", "z", "y")
    x_size, c_size, z_size, y_size = (lax.axis_size(a) for a in axes)
    channels = row_size * col_size
    own = transform(strain, offsets, bins)

    column = [own] + fetch_all(own, "z", z_size)
    right = [own] + fetch_all(own, "x", x_size)
    other = fetch_all(own, "y", y_size)
    near = functools.reduce(jnp.add, [energy_of(w) for w in column])
    column, right, other, near = lax.optimization_barrier((column, right, other, near))

    forward = [fetch(w, "y", y_size, step) for w in column[1:] for step in range(1, y_size)]
    far = []
    for i in range(1, x_size):
        for j in range(y_size):
            pairs = [
                (partners(x_size)[i](x) * y_size + partners(y_size)[j](y), x * y_size + y)
                for x in range(x_size)
                for y in range(y_size)
            ]
            far.append(lax.ppermute(near, ("x", "y"), pairs))
    forward, far, near = lax.optimization_barrier((forward, far, near))
    energy = functools.reduce(jnp.add, [energy_of(w) for w in other + forward], near)
    energy = functools.reduce(jnp.add, far, energy)

    energy = functools.reduce(jnp.add, fetch_all(energy, "c", c_size), energy)
    right = right + [fetch(w, "c", c_size, step) for step in range(1, c_size) for w in right]
    x, c, z, y = (lax.axis_index(a) for a in axes)
    across = [f(x) * c_size + g(c) for g in partners(c_size) for f in partners(x_size)]
    up = [f(z) * y_size + y for f in partners(z_size)]
    up = up + [z * y_size + g(y) for g in partners(y_size)[1:]]
    up = up + [f(z) * y_size + g(y) for f in partners(z_size)[1:] for g in partners(y_size)[1:]]
    places = jnp.stack(across + up).astype(jnp.int32)
    left = column + other + forward
    return cross(places, energy, left, right, offsets.shape[0], bins.shape[0], channels)


def factors(size):
    return (size // 2, 2) if size % 2 == 0 else (size, 1)


def solution(mesh):
    row_size, col_size = mesh.shape["row"], mesh.shape["col"]
    shape = factors(row_size) + factors(col_size)
    fine = Mesh(mesh.devices.reshape(shape), ("x", "c", "z", "y"))
    return jax.shard_map(
        functools.partial(per_device, row_size, col_size),
        mesh=fine,
        in_specs=(P(("x", "c", "z", "y"), None), P(), P()),
        out_specs=P(("x", "c"), None, ("z", "y"), None, None),
        check_vma=False,
    )
```

```python
import functools
import math

import jax
import jax.numpy as jnp
from jax import lax
from jax.experimental import pallas as pl
from jax.experimental.pallas import tpu as pltpu
from jax.sharding import Mesh
from jax.sharding import PartitionSpec as P

SEGLEN = 6000
TAPER = 32
SMOOTH = 64
EPS = 1e-06
LANES = 128
DEPTH = 256
VMEM_LIMIT = 58 << 20
CROSS_VMEM = 16 << 20
EXTRA = 16
PIECES = 3
EDGE = 16


def turns_of(place):
    return place.astype(jnp.float32) * (2.0 * math.pi / SEGLEN)


def transform_kernel(
    count, rows, width, offsets_hbm, strain_hbm, bins_hbm, payload,
    offsets, strain, bins, trig, record, shift, blocks, sums, parts, table, waves, sems,
):
    arrivals = [
        pltpu.make_async_copy(source, target, sems.at[i])
        for i, (source, target) in enumerate(
            [(bins_hbm, bins), (offsets_hbm, offsets), (strain_hbm, strain)]
        )
    ]
    for copy in arrivals:
        copy.start()

    arrivals[0].wait()
    high_rows = DEPTH // EDGE
    twist_row = EDGE + high_rows
    mult_row = lax.broadcasted_iota(jnp.int32, (twist_row + rows, 1), 0)
    mult = jnp.where(
        mult_row < EDGE,
        mult_row,
        jnp.where(mult_row < twist_row, (mult_row - EDGE) * EDGE, (mult_row - twist_row) * DEPTH),
    ).astype(jnp.float32)
    phase = mult * bins[...].reshape(1, width).astype(jnp.float32)
    turns = jnp.floor(phase * (1.0 / SEGLEN) + 0.5)
    angle = turns_of(phase - turns * SEGLEN)
    waves[0] = jnp.cos(angle)
    waves[1] = jnp.sin(angle)
    tiles = width // LANES
    low_cos = waves[0, 0:EDGE, :]
    low_sin = waves[1, 0:EDGE, :]
    for high in range(high_rows):
        at = EDGE + high
        high_cos = waves[0, at : at + 1, :]
        high_sin = waves[1, at : at + 1, :]
        real = high_cos * low_cos - high_sin * low_sin
        imag = -(high_sin * low_cos + high_cos * low_sin)
        for tile in range(tiles):
            cut = slice(tile * LANES, (tile + 1) * LANES)
            to = 2 * tile * LANES
            here = slice(high * EDGE, (high + 1) * EDGE)
            table[here, to : to + LANES] = real[:, cut].astype(jnp.bfloat16)
            table[here, to + LANES : to + 2 * LANES] = imag[:, cut].astype(jnp.bfloat16)
    line = lax.broadcasted_iota(jnp.int32, (rows, DEPTH), 0)
    turn = turns_of(line * DEPTH + lax.broadcasted_iota(jnp.int32, (rows, DEPTH), 1))
    trig[0] = 0.5 * jnp.cos(turn)
    trig[1] = 0.5 * jnp.sin(turn)
    arrivals[1].wait()
    for s in range(count):
        inside = (offsets[s] & (LANES - 1)).astype(jnp.float32)
        shift[0, s : s + 1, :] = jnp.full((1, LANES), inside, jnp.float32)
    turn = turns_of(shift[0])
    shift[1] = jnp.cos(turn)
    shift[2] = jnp.sin(turn)
    for copy in arrivals[2:]:
        copy.wait()
    samples = strain.shape[1]
    chunk = LANES * 8 * 8
    begin = 0
    while begin < samples:
        size = min(chunk, samples - begin)
        part = strain[:, begin : begin + size].astype(jnp.float32)
        record[begin // LANES : (begin + size) // LANES, :] = part.reshape(size // LANES, LANES)
        begin += size
    tail = record.shape[0] - samples // LANES
    record[samples // LANES :, :] = jnp.zeros((tail, LANES), jnp.float32)
    place = (
        lax.broadcasted_iota(jnp.int32, (8, LANES), 0) * DEPTH
        + lax.broadcasted_iota(jnp.int32, (8, LANES), 1)
    ).astype(jnp.float32)
    steps = DEPTH // LANES
    for s in range(count):
        first = offsets[s] // LANES
        moved = place - shift[0, s : s + 1, :]
        turn_cos = shift[1, s : s + 1, :]
        turn_sin = shift[2, s : s + 1, :]
        total = jnp.zeros((8, LANES), jnp.float32)
        for start in range(0, rows, 8):
            here = slice(start, start + 8)
            for part in range(steps):
                lanes = slice(part * LANES, (part + 1) * LANES)
                block = record[pl.ds(first + part + steps * start, 8, stride=steps), :]
                window = 0.5 - (trig[0, here, lanes] * turn_cos + trig[1, here, lanes] * turn_sin)
                value = block * window
                sample = start * DEPTH + part * LANES
                if sample == 0:
                    value = jnp.where(moved > -0.5, value, 0.0)
                if (start + 7) * DEPTH + (part + 1) * LANES > SEGLEN:
                    value = jnp.where(moved < SEGLEN - sample - 0.5, value, 0.0)
                value = value.astype(jnp.bfloat16).astype(jnp.float32)
                total = total + value * value
                blocks[part, pl.ds(s + start * count, 8, stride=count), :] = value
        sums[s : s + 1, :] = jnp.sum(total, axis=0, keepdims=True)
    tapered = jnp.concatenate(
        [blocks[part].astype(jnp.bfloat16) for part in range(steps)], axis=1
    )
    lane = lax.broadcasted_iota(jnp.int32, (count, LANES), 1)
    line = lax.broadcasted_iota(jnp.int32, (count, LANES), 0)
    whole = jnp.sum(sums[...], axis=1, keepdims=True)
    rest = jnp.sum(jnp.where(lane == line, whole, 0.0), axis=0, keepdims=True)
    place = lax.broadcasted_iota(jnp.int32, (EXTRA, LANES), 0)
    extra = jnp.zeros((EXTRA, LANES), jnp.float32)
    for i in range(PIECES):
        piece = rest.astype(jnp.bfloat16).astype(jnp.float32)
        extra = jnp.where(place == i, piece, extra)
        rest = rest - piece
    payload[2 * tiles * count :, :] = extra.astype(jnp.bfloat16)

    for tile in range(tiles):
        cut = slice(tile * LANES, (tile + 1) * LANES)
        to = 2 * tile * LANES
        product = jnp.dot(
            tapered, table[:, to : to + 2 * LANES], preferred_element_type=jnp.float32
        )
        real = jnp.zeros((count, LANES), jnp.float32)
        imag = jnp.zeros((count, LANES), jnp.float32)
        for r in range(rows):
            part = product[r * count : (r + 1) * count, :]
            twist_re = waves[0, twist_row + r : twist_row + r + 1, cut]
            twist_im = -waves[1, twist_row + r : twist_row + r + 1, cut]
            part_re, part_im = part[:, :LANES], part[:, LANES:]
            real = real + (part_re * twist_re - part_im * twist_im)
            imag = imag + (part_re * twist_im + part_im * twist_re)
        parts[0, :, cut] = real
        parts[1, :, cut] = imag
    real, imag = parts[0], parts[1]
    power = real * real + imag * imag
    reach = 1
    while reach < SMOOTH // 4:
        power = power + sum(pltpu.roll(power, width - k * reach, 1) for k in range(1, 4))
        reach *= 4
    power = sum(pltpu.roll(power, (SMOOTH // 2 - k * reach) % width, 1) for k in range(4))
    lane = lax.broadcasted_iota(jnp.int32, (count, width), 1)
    begin, end = SMOOTH // 2, width - SMOOTH // 2
    power = jnp.where(lane < begin, power[:, begin : begin + 1], power)
    power = jnp.where(lane > end, power[:, end : end + 1], power)
    bin_at = (lax.broadcasted_iota(jnp.int32, (1, width), 1)).astype(jnp.float32) + 0.5
    rise = jnp.minimum(jnp.minimum(bin_at, width - bin_at) * (1.0 / TAPER), 1.0)
    ramp = jnp.square(jnp.sin(0.5 * math.pi * rise))
    scale = ramp * lax.rsqrt(power * (1.0 / SMOOTH) + EPS)
    real, imag = (real * scale).astype(jnp.bfloat16), (imag * scale).astype(jnp.bfloat16)
    for tile in range(tiles):
        cut = slice(tile * LANES, (tile + 1) * LANES)
        payload[2 * tile * count : (2 * tile + 1) * count, :] = real[:, cut]
        payload[(2 * tile + 1) * count : (2 * tile + 2) * count, :] = imag[:, cut]


def transform(strain, offsets, bins):
    count, width = offsets.shape[0], bins.shape[0]
    samples = strain.shape[1]
    rows = -(-(SEGLEN + LANES - 1) // (8 * DEPTH)) * 8
    lines = -(-(samples // LANES + DEPTH // LANES) // 8) * 8
    vmem = pl.BlockSpec(memory_space=pltpu.VMEM)
    hbm = pl.BlockSpec(memory_space=pltpu.HBM)
    return pl.pallas_call(
        functools.partial(transform_kernel, count, rows, width),
        out_shape=jax.ShapeDtypeStruct((2 * width // LANES * count + EXTRA, LANES), jnp.bfloat16),
        in_specs=[hbm] * 3,
        out_specs=vmem,
        scratch_shapes=[
            pltpu.SMEM(offsets.shape, jnp.int32),
            pltpu.VMEM(strain.shape, strain.dtype),
            pltpu.VMEM(bins.shape, jnp.int32),
            pltpu.VMEM((2, rows, DEPTH), jnp.float32),
            pltpu.VMEM((lines, LANES), jnp.float32),
            pltpu.VMEM((3, count, LANES), jnp.float32),
            pltpu.VMEM((DEPTH // LANES, rows * count, LANES), jnp.float32),
            pltpu.VMEM((count, LANES), jnp.float32),
            pltpu.VMEM((2, count, width), jnp.float32),
            pltpu.VMEM((DEPTH, 2 * width), jnp.bfloat16),
            pltpu.VMEM((2, EDGE + DEPTH // EDGE + rows, width), jnp.float32),
            pltpu.SemaphoreType.DMA((3,)),
        ],
        compiler_params=pltpu.CompilerParams(vmem_limit_bytes=VMEM_LIMIT),
        cost_estimate=pl.CostEstimate(flops=400 << 20, bytes_accessed=6 << 20, transcendentals=0),
        name="transform",
    )(offsets, strain, bins)


def energy_of(payload):
    return jnp.sum(payload[-EXTRA:, :].astype(jnp.float32), axis=0, keepdims=True)


def share_of(energy, count, channels):
    lane = lax.broadcasted_iota(jnp.int32, (count, LANES), 1)
    line = lax.broadcasted_iota(jnp.int32, (count, LANES), 0)
    weight = 1.0 / (energy * (1.0 / (channels * SEGLEN)) + EPS)
    weight = jnp.where(lane[0:1] < count, weight, 0.0)
    weight = weight / jnp.sum(weight, axis=1, keepdims=True)
    column = jnp.sum(jnp.where(lane == line, weight, 0.0), axis=1, keepdims=True)
    return jnp.broadcast_to(column, (count, LANES))


def cross_kernel(left_count, right_count, count, channels, places, energy, *refs):
    left, right = refs[:left_count], refs[left_count : left_count + right_count]
    out, block, sems = refs[left_count + right_count :]
    share = share_of(energy[...], count, channels)
    tiles = block.shape[-1] // LANES
    copies = [
        pltpu.make_async_copy(block.at[i], out.at[places[right_count + i]], sems.at[i])
        for i in range(left_count)
    ]
    for i, ref in enumerate(left):
        for tile in range(tiles):
            cut = slice(tile * LANES, (tile + 1) * LANES)
            at_re = slice(2 * tile * count, (2 * tile + 1) * count)
            at_im = slice((2 * tile + 1) * count, (2 * tile + 2) * count)
            left_re = ref[at_re, :].astype(jnp.float32) * share
            left_im = ref[at_im, :].astype(jnp.float32) * share
            for j, other in enumerate(right):
                right_re = other[at_re, :].astype(jnp.float32)
                right_im = other[at_im, :].astype(jnp.float32)
                real = left_re * right_re + left_im * right_im
                imag = left_im * right_re - left_re * right_im
                at = places[j]
                block[i, at, 0, 0:1, cut] = jnp.sum(real, axis=0, keepdims=True)
                block[i, at, 0, 1:2, cut] = jnp.sum(imag, axis=0, keepdims=True)
        copies[i].start()
    for copy in copies:
        copy.wait()


def cross(places, energy, left, right, count, width, channels):
    vmem = pl.BlockSpec(memory_space=pltpu.VMEM)
    arrays = [energy, *left, *right]
    return pl.pallas_call(
        functools.partial(cross_kernel, len(left), len(right), count, channels),
        out_shape=jax.ShapeDtypeStruct((len(left), len(right), 1, 2, width), jnp.float32),
        in_specs=[pl.BlockSpec(memory_space=pltpu.SMEM)] + [vmem] * len(arrays),
        out_specs=pl.BlockSpec(memory_space=pltpu.HBM),
        scratch_shapes=[
            pltpu.VMEM((len(left), len(right), 1, 2, width), jnp.float32),
            pltpu.SemaphoreType.DMA((len(left),)),
        ],
        compiler_params=pltpu.CompilerParams(vmem_limit_bytes=CROSS_VMEM),
        cost_estimate=pl.CostEstimate(flops=4 << 20, bytes_accessed=2 << 20, transcendentals=0),
        name="cross",
    )(places, *arrays)


def partners(size):
    if size & (size - 1) == 0:
        return [lambda p, k=k: p ^ k for k in range(size)]
    return [lambda p, k=k: (p - k) % size for k in range(size)]


def fetch(x, axis, size, step):
    source = partners(size)[step]
    return lax.ppermute(x, axis, [(source(p), p) for p in range(size)])


def fetch_all(x, axis, size):
    return [fetch(x, axis, size, step) for step in range(size - 1, 0, -1)][::-1]


def per_device(row_size, col_size, strain, offsets, bins):
    axes = ("x", "c", "z", "y")
    x_size, c_size, z_size, y_size = (lax.axis_size(a) for a in axes)
    channels = row_size * col_size
    own = transform(strain, offsets, bins)

    column = [own] + fetch_all(own, "z", z_size)
    beside = fetch_all(own, "x", x_size)
    other = fetch_all(own, "y", y_size)
    soon = [fetch(w, "y", y_size, step) for w in column[3:] for step in range(1, y_size)]
    other, beside, soon, column = lax.optimization_barrier((other, beside, soon, column))
    near = functools.reduce(jnp.add, [energy_of(w) for w in column])

    forward = [fetch(w, "y", y_size, step) for w in column[1:3] for step in range(1, y_size)]
    far = []
    for i in range(1, x_size):
        for j in range(y_size):
            pairs = [
                (partners(x_size)[i](x) * y_size + partners(y_size)[j](y), x * y_size + y)
                for x in range(x_size)
                for y in range(y_size)
            ]
            far.append(lax.ppermute(near, ("x", "y"), pairs))
    forward, far, near = lax.optimization_barrier((forward, far, near))
    forward = forward + soon
    energy = functools.reduce(jnp.add, [energy_of(w) for w in other + forward], near)
    energy = functools.reduce(jnp.add, far, energy)

    energy = functools.reduce(jnp.add, fetch_all(energy, "c", c_size), energy)
    right = [own] + beside
    right = right + [fetch(w, "c", c_size, step) for step in range(1, c_size) for w in right]
    x, c, z, y = (lax.axis_index(a) for a in axes)
    across = [f(x) * c_size + g(c) for g in partners(c_size) for f in partners(x_size)]
    up = [f(z) * y_size + y for f in partners(z_size)]
    up = up + [z * y_size + g(y) for g in partners(y_size)[1:]]
    up = up + [f(z) * y_size + g(y) for f in partners(z_size)[1:] for g in partners(y_size)[1:]]
    places = jnp.stack(across + up).astype(jnp.int32)
    left = column + other + forward
    return cross(places, energy, left, right, offsets.shape[0], bins.shape[0], channels)


def factors(size):
    return (size // 2, 2) if size % 2 == 0 else (size, 1)


def solution(mesh):
    row_size, col_size = mesh.shape["row"], mesh.shape["col"]
    shape = factors(row_size) + factors(col_size)
    fine = Mesh(mesh.devices.reshape(shape), ("x", "c", "z", "y"))
    return jax.shard_map(
        functools.partial(per_device, row_size, col_size),
        mesh=fine,
        in_specs=(P(("x", "c", "z", "y"), None), P(), P()),
        out_specs=P(("x", "c"), None, ("z", "y"), None, None),
        check_vma=False,
    )
```

```python
import functools
import math

import jax
import jax.numpy as jnp
from jax import lax
from jax.experimental import pallas as pl
from jax.experimental.pallas import tpu as pltpu
from jax.sharding import Mesh
from jax.sharding import PartitionSpec as P

SEGLEN = 6000
TAPER = 32
SMOOTH = 64
EPS = 1e-06
LANES = 128
DEPTH = 256
VMEM_LIMIT = 58 << 20
CROSS_VMEM = 16 << 20
PRODUCT_BYTES = 8 << 20
EXTRA = 16
PIECES = 3
EDGE = 16


def turns_of(place):
    return place.astype(jnp.float32) * (2.0 * math.pi / SEGLEN)


def transform_kernel(
    count, rows, width, offsets_hbm, strain_hbm, bins_hbm, payload,
    offsets, strain, bins, trig, ramp, record, shift, blocks, sums, table, waves, sems,
):
    arrivals = [
        pltpu.make_async_copy(source, target, sems.at[i])
        for i, (source, target) in enumerate(
            [(bins_hbm, bins), (offsets_hbm, offsets), (strain_hbm, strain)]
        )
    ]
    for copy in arrivals:
        copy.start()

    line = lax.broadcasted_iota(jnp.int32, (rows, DEPTH), 0)
    turn = turns_of(line * DEPTH + lax.broadcasted_iota(jnp.int32, (rows, DEPTH), 1))
    trig[0] = 0.5 * jnp.cos(turn)
    trig[1] = 0.5 * jnp.sin(turn)
    bin_at = lax.broadcasted_iota(jnp.int32, (1, width), 1).astype(jnp.float32) + 0.5
    rise = jnp.minimum(jnp.minimum(bin_at, width - bin_at) * (1.0 / TAPER), 1.0)
    ramp[...] = jnp.square(jnp.sin(0.5 * math.pi * rise))

    arrivals[0].wait()
    high_rows = DEPTH // EDGE
    twist_row = EDGE + high_rows
    mult_row = lax.broadcasted_iota(jnp.int32, (twist_row + rows, 1), 0)
    mult = jnp.where(
        mult_row < EDGE,
        mult_row,
        jnp.where(mult_row < twist_row, (mult_row - EDGE) * EDGE, (mult_row - twist_row) * DEPTH),
    ).astype(jnp.float32)
    phase = mult * bins[...].reshape(1, width).astype(jnp.float32)
    turns = jnp.floor(phase * (1.0 / SEGLEN) + 0.5)
    angle = turns_of(phase - turns * SEGLEN)
    waves[0] = jnp.cos(angle)
    waves[1] = jnp.sin(angle)
    tiles = width // LANES
    low_cos = waves[0, 0:EDGE, :]
    low_sin = waves[1, 0:EDGE, :]
    for high in range(high_rows):
        at = EDGE + high
        high_cos = waves[0, at : at + 1, :]
        high_sin = waves[1, at : at + 1, :]
        real = high_cos * low_cos - high_sin * low_sin
        imag = -(high_sin * low_cos + high_cos * low_sin)
        for tile in range(tiles):
            cut = slice(tile * LANES, (tile + 1) * LANES)
            to = 2 * tile * LANES
            here = slice(high * EDGE, (high + 1) * EDGE)
            table[here, to : to + LANES] = real[:, cut].astype(jnp.bfloat16)
            table[here, to + LANES : to + 2 * LANES] = imag[:, cut].astype(jnp.bfloat16)
    arrivals[1].wait()
    for s in range(count):
        inside = (offsets[s] & (LANES - 1)).astype(jnp.float32)
        shift[0, s : s + 1, :] = jnp.full((1, LANES), inside, jnp.float32)
    turn = turns_of(shift[0])
    shift[1] = jnp.cos(turn)
    shift[2] = jnp.sin(turn)
    for copy in arrivals[2:]:
        copy.wait()
    samples = strain.shape[1]
    chunk = LANES * 8 * 8
    begin = 0
    while begin < samples:
        size = min(chunk, samples - begin)
        part = strain[:, begin : begin + size].astype(jnp.float32)
        record[begin // LANES : (begin + size) // LANES, :] = part.reshape(size // LANES, LANES)
        begin += size
    tail = record.shape[0] - samples // LANES
    record[samples // LANES :, :] = jnp.zeros((tail, LANES), jnp.float32)
    place = (
        lax.broadcasted_iota(jnp.int32, (8, LANES), 0) * DEPTH
        + lax.broadcasted_iota(jnp.int32, (8, LANES), 1)
    ).astype(jnp.float32)
    steps = DEPTH // LANES
    for s in range(count):
        first = offsets[s] // LANES
        moved = place - shift[0, s : s + 1, :]
        turn_cos = shift[1, s : s + 1, :]
        turn_sin = shift[2, s : s + 1, :]
        total = jnp.zeros((8, LANES), jnp.float32)
        for start in range(0, rows, 8):
            here = slice(start, start + 8)
            for part in range(steps):
                lanes = slice(part * LANES, (part + 1) * LANES)
                block = record[pl.ds(first + part + steps * start, 8, stride=steps), :]
                window = 0.5 - (trig[0, here, lanes] * turn_cos + trig[1, here, lanes] * turn_sin)
                value = block * window
                sample = start * DEPTH + part * LANES
                if sample == 0:
                    value = jnp.where(moved > -0.5, value, 0.0)
                if (start + 7) * DEPTH + (part + 1) * LANES > SEGLEN:
                    value = jnp.where(moved < SEGLEN - sample - 0.5, value, 0.0)
                value = value.astype(jnp.bfloat16).astype(jnp.float32)
                total = total + value * value
                blocks[part, pl.ds(s + start * count, 8, stride=count), :] = value
        sums[s : s + 1, :] = jnp.sum(total, axis=0, keepdims=True)
    tapered = jnp.concatenate(
        [blocks[part].astype(jnp.bfloat16) for part in range(steps)], axis=1
    )

    def window_sums(tile):
        above = powers[min(tile + 1, tiles - 1)]
        sums = jnp.concatenate([powers[tile], above], axis=1)
        reach = 1
        while reach < SMOOTH:
            sums = sums + sum(pltpu.roll(sums, 2 * LANES - k * reach, 1) for k in range(1, 4))
            reach *= 4
        return pltpu.roll(sums[:, :LANES], SMOOTH // 2, 1)

    def whiten(tile):
        windows.append(window_sums(tile))
        lane = lax.broadcasted_iota(jnp.int32, (count, LANES), 1)
        begin, end = SMOOTH // 2, LANES - SMOOTH // 2
        under = windows[tile][:, begin : begin + 1] if tile == 0 else windows[tile - 1]
        power = jnp.where(lane < begin, under, windows[tile])
        if tile == tiles - 1:
            power = jnp.where(lane > end, power[:, end : end + 1], power)
        cut = slice(tile * LANES, (tile + 1) * LANES)
        scale = ramp[:, cut] * lax.rsqrt(power * (1.0 / SMOOTH) + EPS)
        real, imag = spectra[tile]
        at = 2 * tile * count
        payload[at : at + count, :] = (real * scale).astype(jnp.bfloat16)
        payload[at + count : at + 2 * count, :] = (imag * scale).astype(jnp.bfloat16)

    def write_energy():
        lane = lax.broadcasted_iota(jnp.int32, (count, LANES), 1)
        line = lax.broadcasted_iota(jnp.int32, (count, LANES), 0)
        whole = jnp.sum(sums[...], axis=1, keepdims=True)
        rest = jnp.sum(jnp.where(lane == line, whole, 0.0), axis=0, keepdims=True)
        place = lax.broadcasted_iota(jnp.int32, (EXTRA, LANES), 0)
        extra = jnp.zeros((EXTRA, LANES), jnp.float32)
        for i in range(PIECES):
            piece = rest.astype(jnp.bfloat16).astype(jnp.float32)
            extra = jnp.where(place == i, piece, extra)
            rest = rest - piece
        payload[2 * tiles * count :, :] = extra.astype(jnp.bfloat16)
    spectra, powers, windows = [], [], []
    for tile in range(tiles):
        cut = slice(tile * LANES, (tile + 1) * LANES)
        to = 2 * tile * LANES
        product = jnp.dot(
            tapered, table[:, to : to + 2 * LANES], preferred_element_type=jnp.float32
        )
        real = jnp.zeros((count, LANES), jnp.float32)
        imag = jnp.zeros((count, LANES), jnp.float32)
        for r in range(rows):
            part = product[r * count : (r + 1) * count, :]
            twist_re = waves[0, twist_row + r : twist_row + r + 1, cut]
            twist_im = -waves[1, twist_row + r : twist_row + r + 1, cut]
            part_re, part_im = part[:, :LANES], part[:, LANES:]
            real = real + (part_re * twist_re - part_im * twist_im)
            imag = imag + (part_re * twist_im + part_im * twist_re)
        spectra.append((real, imag))
        powers.append(real * real + imag * imag)
        if tile == 0:
            write_energy()
        else:
            whiten(tile - 1)
    whiten(tiles - 1)


def transform(strain, offsets, bins):
    count, width = offsets.shape[0], bins.shape[0]
    samples = strain.shape[1]
    rows = -(-(SEGLEN + LANES - 1) // (8 * DEPTH)) * 8
    lines = -(-(samples // LANES + DEPTH // LANES) // 8) * 8
    vmem = pl.BlockSpec(memory_space=pltpu.VMEM)
    hbm = pl.BlockSpec(memory_space=pltpu.HBM)
    return pl.pallas_call(
        functools.partial(transform_kernel, count, rows, width),
        out_shape=jax.ShapeDtypeStruct((2 * width // LANES * count + EXTRA, LANES), jnp.bfloat16),
        in_specs=[hbm] * 3,
        out_specs=vmem,
        scratch_shapes=[
            pltpu.SMEM(offsets.shape, jnp.int32),
            pltpu.VMEM(strain.shape, strain.dtype),
            pltpu.VMEM(bins.shape, jnp.int32),
            pltpu.VMEM((2, rows, DEPTH), jnp.float32),
            pltpu.VMEM((1, width), jnp.float32),
            pltpu.VMEM((lines, LANES), jnp.float32),
            pltpu.VMEM((3, count, LANES), jnp.float32),
            pltpu.VMEM((DEPTH // LANES, rows * count, LANES), jnp.float32),
            pltpu.VMEM((count, LANES), jnp.float32),
            pltpu.VMEM((DEPTH, 2 * width), jnp.bfloat16),
            pltpu.VMEM((2, EDGE + DEPTH // EDGE + rows, width), jnp.float32),
            pltpu.SemaphoreType.DMA((3,)),
        ],
        compiler_params=pltpu.CompilerParams(vmem_limit_bytes=VMEM_LIMIT),
        cost_estimate=pl.CostEstimate(flops=400 << 20, bytes_accessed=6 << 20, transcendentals=0),
        name="transform",
    )(offsets, strain, bins)


def energy_of(payload):
    return jnp.sum(payload[-EXTRA:, :].astype(jnp.float32), axis=0, keepdims=True)


def weights_of(energy, count, channels):
    lane = lax.broadcasted_iota(jnp.int32, (count, LANES), 1)
    line = lax.broadcasted_iota(jnp.int32, (count, LANES), 0)
    weight = 1.0 / (energy * (1.0 / (channels * SEGLEN)) + EPS)
    weight = jnp.where(lane[0:1] < count, weight, 0.0)
    scale = 1.0 / jnp.sum(weight, axis=1, keepdims=True)
    column = jnp.sum(jnp.where(lane == line, weight, 0.0), axis=1, keepdims=True)
    return jnp.broadcast_to(column, (count, LANES)), scale


AXES = ("x", "c", "z", "y")


def places_here():
    x_size, c_size, z_size, y_size = (lax.axis_size(a) for a in AXES)
    x, c, z, y = (lax.axis_index(a) for a in AXES)
    across = [f(x) * c_size + g(c) for g in partners(c_size) for f in partners(x_size)]
    up = [f(z) * y_size + y for f in partners(z_size)]
    up = up + [z * y_size + g(y) for g in partners(y_size)[1:]]
    up = up + [f(z) * y_size + g(y) for f in partners(z_size)[1:] for g in partners(y_size)[1:]]
    return up, across


def cross_kernel(left_count, right_count, count, channels, energy, *refs):
    left, right = refs[:left_count], refs[left_count : left_count + right_count]
    out, block, sems = refs[left_count + right_count :]
    weight, scale = weights_of(energy[...], count, channels)
    share = weight * scale
    up, across = places_here()
    copies = []
    for tile in range(block.shape[-1] // LANES):
        cut = slice(tile * LANES, (tile + 1) * LANES)
        at_re = slice(2 * tile * count, (2 * tile + 1) * count)
        at_im = slice((2 * tile + 1) * count, (2 * tile + 2) * count)
        rights = [
            (ref[at_re, :].astype(jnp.float32), ref[at_im, :].astype(jnp.float32)) for ref in right
        ]
        for i, ref in enumerate(left):
            left_re = ref[at_re, :].astype(jnp.float32) * share
            left_im = ref[at_im, :].astype(jnp.float32) * share
            for j, (right_re, right_im) in enumerate(rights):
                real = left_re * right_re + left_im * right_im
                imag = left_im * right_re - left_re * right_im
                at = up[i], across[j]
                block[at[0], at[1], 0, 0:1, cut] = jnp.sum(real, axis=0, keepdims=True)
                block[at[0], at[1], 0, 1:2, cut] = jnp.sum(imag, axis=0, keepdims=True)
        part = (slice(None),) * 4 + (cut,)
        copies.append(pltpu.make_async_copy(block.at[part], out.at[part], sems.at[tile]))
        copies[-1].start()
    for copy in copies:
        copy.wait()


def cross(energy, left, right, count, width, channels):
    vmem = pl.BlockSpec(memory_space=pltpu.VMEM)
    arrays = [energy, *left, *right]
    return pl.pallas_call(
        functools.partial(cross_kernel, len(left), len(right), count, channels),
        out_shape=jax.ShapeDtypeStruct((len(left), len(right), 1, 2, width), jnp.float32),
        in_specs=[vmem] * len(arrays),
        out_specs=pl.BlockSpec(memory_space=pltpu.HBM),
        scratch_shapes=[
            pltpu.VMEM((len(left), len(right), 1, 2, width), jnp.float32),
            pltpu.SemaphoreType.DMA((width // LANES,)),
        ],
        compiler_params=pltpu.CompilerParams(vmem_limit_bytes=CROSS_VMEM),
        cost_estimate=pl.CostEstimate(flops=4 << 20, bytes_accessed=2 << 20, transcendentals=0),
        name="cross",
    )(*arrays)


def product_kernel(left_count, right_count, count, *refs):
    left, right = refs[:left_count], refs[left_count : left_count + right_count]
    products = refs[-1]
    for tile in range(products.shape[1] // 2):
        at_re = slice(2 * tile * count, (2 * tile + 1) * count)
        at_im = slice((2 * tile + 1) * count, (2 * tile + 2) * count)
        rights = [
            (ref[at_re, :].astype(jnp.float32), ref[at_im, :].astype(jnp.float32)) for ref in right
        ]
        for i, ref in enumerate(left):
            left_re = ref[at_re, :].astype(jnp.float32)
            left_im = ref[at_im, :].astype(jnp.float32)
            for j, (right_re, right_im) in enumerate(rights):
                pair = i * right_count + j
                products[pair, 2 * tile] = left_re * right_re + left_im * right_im
                products[pair, 2 * tile + 1] = left_im * right_re - left_re * right_im


def pair_products(left, right, count, width):
    pairs = len(left) * len(right)
    vmem = pl.BlockSpec(memory_space=pltpu.VMEM)
    return pl.pallas_call(
        functools.partial(product_kernel, len(left), len(right), count),
        out_shape=jax.ShapeDtypeStruct((pairs, 2 * width // LANES, count, LANES), jnp.float32),
        in_specs=[vmem] * (len(left) + len(right)),
        out_specs=vmem,
        compiler_params=pltpu.CompilerParams(vmem_limit_bytes=CROSS_VMEM),
        cost_estimate=pl.CostEstimate(flops=4 << 20, bytes_accessed=2 << 20, transcendentals=0),
        name="pair_products",
    )(*left, *right)


def sublane_sums(values):
    row = lax.broadcasted_iota(jnp.int32, (8, LANES), 0)
    for bit in (4, 2, 1):
        low = (row & bit) == 0
        packed = []
        for q in range(bit):
            a, b = values[q], values[q + bit]
            theirs = jnp.where(low, b, a)
            down = pltpu.roll(theirs, bit, 0)
            if bit < 4:
                down = jnp.where(low, pltpu.roll(theirs, 8 - bit, 0), down)
            packed.append(jnp.where(low, a, b) + down)
        values = packed
    return values[0]


def stack_kernel(left_count, right_count, channels, energy, products, out, block, sems):
    count = products.shape[2]
    weight, scale = weights_of(energy[...], count, channels)
    up, across = places_here()
    copies = []
    for tile in range(block.shape[-1] // LANES):
        cut = slice(tile * LANES, (tile + 1) * LANES)
        for i in range(left_count):
            at = up[i]
            for first in range(0, right_count, 4):
                some = range(first, min(first + 4, right_count))
                sums = []
                for j in some:
                    for part in range(2):
                        total = jnp.zeros((8, LANES), jnp.float32)
                        for begin in range(0, count, 8):
                            here = slice(begin, begin + 8)
                            product = products[i * right_count + j, 2 * tile + part, here, :]
                            total = total + product * weight[here, :]
                        sums.append(total)
                sums = sublane_sums(sums + [sums[0]] * (8 - len(sums))) * scale
                for k, j in enumerate(some):
                    block[at, across[j], 0, :, cut] = sums[2 * k : 2 * k + 2, :]
        part = (slice(None),) * 4 + (cut,)
        copies.append(pltpu.make_async_copy(block.at[part], out.at[part], sems.at[tile]))
        copies[-1].start()
    for copy in copies:
        copy.wait()


def stack(energy, products, left_count, right_count, width, channels):
    vmem = pl.BlockSpec(memory_space=pltpu.VMEM)
    shape = (left_count, right_count, 1, 2, width)
    return pl.pallas_call(
        functools.partial(stack_kernel, left_count, right_count, channels),
        out_shape=jax.ShapeDtypeStruct(shape, jnp.float32),
        in_specs=[vmem, vmem],
        out_specs=pl.BlockSpec(memory_space=pltpu.HBM),
        scratch_shapes=[
            pltpu.VMEM(shape, jnp.float32),
            pltpu.SemaphoreType.DMA((width // LANES,)),
        ],
        compiler_params=pltpu.CompilerParams(vmem_limit_bytes=CROSS_VMEM),
        cost_estimate=pl.CostEstimate(flops=4 << 20, bytes_accessed=2 << 20, transcendentals=0),
        name="stack",
    )(energy, products)


def partners(size):
    if size & (size - 1) == 0:
        return [lambda p, k=k: p ^ k for k in range(size)]
    return [lambda p, k=k: (p - k) % size for k in range(size)]


def fetch(x, axis, size, step):
    source = partners(size)[step]
    return lax.ppermute(x, axis, [(source(p), p) for p in range(size)])


def fetch_all(x, axis, size):
    return [fetch(x, axis, size, step) for step in range(size - 1, 0, -1)][::-1]


def per_device(row_size, col_size, strain, offsets, bins):
    x_size, c_size, z_size, y_size = (lax.axis_size(a) for a in AXES)
    channels = row_size * col_size
    own = transform(strain, offsets, bins)

    column = [own] + fetch_all(own, "z", z_size)
    beside = fetch_all(own, "x", x_size)
    other = fetch_all(own, "y", y_size)
    soon = [fetch(w, "y", y_size, step) for w in column[3:] for step in range(1, y_size)]
    kept = own.astype(jnp.float32)
    other, beside, soon, column, kept = lax.optimization_barrier((other, beside, soon, column, kept))
    near = functools.reduce(jnp.add, [energy_of(w) for w in column[1:]], energy_of(kept))

    forward = [fetch(w, "y", y_size, step) for w in column[1:3] for step in range(1, y_size)]
    far = []
    for i in range(1, x_size):
        for j in range(y_size):
            pairs = [
                (partners(x_size)[i](x) * y_size + partners(y_size)[j](y), x * y_size + y)
                for x in range(x_size)
                for y in range(y_size)
            ]
            far.append(lax.ppermute(near, ("x", "y"), pairs))
    forward, far, near = lax.optimization_barrier((forward, far, near))
    forward = forward + soon
    energy = functools.reduce(jnp.add, [energy_of(w) for w in other + forward], near)
    energy = functools.reduce(jnp.add, far, energy)

    right = [kept] + beside
    right = right + [fetch(w, "c", c_size, step) for step in range(1, c_size) for w in [own] + beside]
    energy, right = lax.optimization_barrier((energy, right))
    energy = functools.reduce(jnp.add, fetch_all(energy, "c", c_size), energy)
    left = [kept] + column[1:] + other + forward
    count, width = offsets.shape[0], bins.shape[0]
    if len(left) * len(right) * count * 2 * width * 4 > PRODUCT_BYTES:
        return cross(energy, left, right, count, width, channels)
    products = pair_products(left, right, count, width)
    return stack(energy, products, len(left), len(right), width, channels)


def factors(size):
    return (size // 2, 2) if size % 2 == 0 else (size, 1)


def solution(mesh):
    row_size, col_size = mesh.shape["row"], mesh.shape["col"]
    shape = factors(row_size) + factors(col_size)
    fine = Mesh(mesh.devices.reshape(shape), AXES)
    return jax.shard_map(
        functools.partial(per_device, row_size, col_size),
        mesh=fine,
        in_specs=(P(("x", "c", "z", "y"), None), P(), P()),
        out_specs=P(("x", "c"), None, ("z", "y"), None, None),
        check_vma=False,
    )
```

```python
import functools
import math

import jax
import jax.numpy as jnp
from jax import lax
from jax.experimental import pallas as pl
from jax.experimental.pallas import tpu as pltpu
from jax.sharding import Mesh
from jax.sharding import PartitionSpec as P

SEGLEN = 6000
TAPER = 32
SMOOTH = 64
EPS = 1e-06
LANES = 128
DEPTH = 256
VMEM_LIMIT = 58 << 20
CROSS_VMEM = 16 << 20
PRODUCT_BYTES = 8 << 20
EXTRA = 16
PIECES = 3
GROUPS = 2
EDGE = 16


def turns_of(place):
    return place.astype(jnp.float32) * (2.0 * math.pi / SEGLEN)


def transform_kernel(
    count, groups, rows, width, offsets_hbm, strain_hbm, bins_hbm, payload,
    offsets, strain, bins, trig, ramp, record, shift, blocks, sums, table, waves, sems,
):
    arrivals = [
        pltpu.make_async_copy(source, target, sems.at[i])
        for i, (source, target) in enumerate(
            [(bins_hbm, bins), (offsets_hbm, offsets), (strain_hbm, strain)]
        )
    ]
    for copy in arrivals:
        copy.start()

    line = lax.broadcasted_iota(jnp.int32, (rows, DEPTH), 0)
    turn = turns_of(line * DEPTH + lax.broadcasted_iota(jnp.int32, (rows, DEPTH), 1))
    trig[0] = 0.5 * jnp.cos(turn)
    trig[1] = 0.5 * jnp.sin(turn)
    bin_at = lax.broadcasted_iota(jnp.int32, (1, width), 1).astype(jnp.float32) + 0.5
    rise = jnp.minimum(jnp.minimum(bin_at, width - bin_at) * (1.0 / TAPER), 1.0)
    ramp[...] = jnp.square(jnp.sin(0.5 * math.pi * rise))

    arrivals[0].wait()
    high_rows = DEPTH // EDGE
    twist_row = EDGE + high_rows
    mult_row = lax.broadcasted_iota(jnp.int32, (twist_row + rows, 1), 0)
    mult = jnp.where(
        mult_row < EDGE,
        mult_row,
        jnp.where(mult_row < twist_row, (mult_row - EDGE) * EDGE, (mult_row - twist_row) * DEPTH),
    ).astype(jnp.float32)
    phase = mult * bins[...].reshape(1, width).astype(jnp.float32)
    turns = jnp.floor(phase * (1.0 / SEGLEN) + 0.5)
    angle = turns_of(phase - turns * SEGLEN)
    waves[0] = jnp.cos(angle)
    waves[1] = jnp.sin(angle)
    tiles = width // LANES
    low_cos = waves[0, 0:EDGE, :]
    low_sin = waves[1, 0:EDGE, :]
    for high in range(high_rows):
        at = EDGE + high
        high_cos = waves[0, at : at + 1, :]
        high_sin = waves[1, at : at + 1, :]
        real = high_cos * low_cos - high_sin * low_sin
        imag = -(high_sin * low_cos + high_cos * low_sin)
        for tile in range(tiles):
            cut = slice(tile * LANES, (tile + 1) * LANES)
            to = 2 * tile * LANES
            here = slice(high * EDGE, (high + 1) * EDGE)
            table[here, to : to + LANES] = real[:, cut].astype(jnp.bfloat16)
            table[here, to + LANES : to + 2 * LANES] = imag[:, cut].astype(jnp.bfloat16)
    arrivals[1].wait()
    for s in range(count):
        inside = (offsets[s] & (LANES - 1)).astype(jnp.float32)
        shift[0, s : s + 1, :] = jnp.full((1, LANES), inside, jnp.float32)
    turn = turns_of(shift[0])
    shift[1] = jnp.cos(turn)
    shift[2] = jnp.sin(turn)
    for copy in arrivals[2:]:
        copy.wait()
    samples = strain.shape[1]
    chunk = LANES * 8 * 8
    begin = 0
    while begin < samples:
        size = min(chunk, samples - begin)
        part = strain[:, begin : begin + size].astype(jnp.float32)
        record[begin // LANES : (begin + size) // LANES, :] = part.reshape(size // LANES, LANES)
        begin += size
    tail = record.shape[0] - samples // LANES
    record[samples // LANES :, :] = jnp.zeros((tail, LANES), jnp.float32)
    place = (
        lax.broadcasted_iota(jnp.int32, (8, LANES), 0) * DEPTH
        + lax.broadcasted_iota(jnp.int32, (8, LANES), 1)
    ).astype(jnp.float32)
    steps = DEPTH // LANES
    some = count // groups

    def taper(group, segments):
        for s in segments:
            first = offsets[s] // LANES
            moved = place - shift[0, s : s + 1, :]
            turn_cos = shift[1, s : s + 1, :]
            turn_sin = shift[2, s : s + 1, :]
            total = jnp.zeros((8, LANES), jnp.float32)
            for start in range(0, rows, 8):
                here = slice(start, start + 8)
                for part in range(steps):
                    lanes = slice(part * LANES, (part + 1) * LANES)
                    block = record[pl.ds(first + part + steps * start, 8, stride=steps), :]
                    window = 0.5 - (trig[0, here, lanes] * turn_cos + trig[1, here, lanes] * turn_sin)
                    value = block * window
                    sample = start * DEPTH + part * LANES
                    if sample == 0:
                        value = jnp.where(moved > -0.5, value, 0.0)
                    if (start + 7) * DEPTH + (part + 1) * LANES > SEGLEN:
                        value = jnp.where(moved < SEGLEN - sample - 0.5, value, 0.0)
                    value = value.astype(jnp.bfloat16).astype(jnp.float32)
                    total = total + value * value
                    at = s - group * some + start * some
                    blocks[group, part, pl.ds(at, 8, stride=some), :] = value
            sums[s : s + 1, :] = jnp.sum(total, axis=0, keepdims=True)

    def tapered_group(group):
        return jnp.concatenate(
            [blocks[group, part].astype(jnp.bfloat16) for part in range(steps)], axis=1
        )

    def window_sums(powers, tile):
        above = powers[min(tile + 1, tiles - 1)]
        sums = jnp.concatenate([powers[tile], above], axis=1)
        reach = 1
        while reach < SMOOTH:
            sums = sums + sum(pltpu.roll(sums, 2 * LANES - k * reach, 1) for k in range(1, 4))
            reach *= 4
        return pltpu.roll(sums[:, :LANES], SMOOTH // 2, 1)

    def whiten(group, spectra, powers, windows, tile):
        windows.append(window_sums(powers, tile))
        lane = lax.broadcasted_iota(jnp.int32, (some, LANES), 1)
        begin, end = SMOOTH // 2, LANES - SMOOTH // 2
        under = windows[tile][:, begin : begin + 1] if tile == 0 else windows[tile - 1]
        power = jnp.where(lane < begin, under, windows[tile])
        if tile == tiles - 1:
            power = jnp.where(lane > end, power[:, end : end + 1], power)
        cut = slice(tile * LANES, (tile + 1) * LANES)
        scale = ramp[:, cut] * lax.rsqrt(power * (1.0 / SMOOTH) + EPS)
        real, imag = spectra[tile]
        at = 2 * tile * count + group * some
        payload[at : at + some, :] = (real * scale).astype(jnp.bfloat16)
        payload[at + count : at + count + some, :] = (imag * scale).astype(jnp.bfloat16)

    def write_energy():
        lane = lax.broadcasted_iota(jnp.int32, (count, LANES), 1)
        line = lax.broadcasted_iota(jnp.int32, (count, LANES), 0)
        whole = jnp.sum(sums[...], axis=1, keepdims=True)
        rest = jnp.sum(jnp.where(lane == line, whole, 0.0), axis=0, keepdims=True)
        place = lax.broadcasted_iota(jnp.int32, (EXTRA, LANES), 0)
        extra = jnp.zeros((EXTRA, LANES), jnp.float32)
        for i in range(PIECES):
            piece = rest.astype(jnp.bfloat16).astype(jnp.float32)
            extra = jnp.where(place == i, piece, extra)
            rest = rest - piece
        payload[2 * tiles * count :, :] = extra.astype(jnp.bfloat16)
    taper(0, range(some))
    for group in range(groups):
        tapered = tapered_group(group)
        spectra, powers, windows = [], [], []
        for tile in range(tiles):
            cut = slice(tile * LANES, (tile + 1) * LANES)
            to = 2 * tile * LANES
            product = jnp.dot(
                tapered, table[:, to : to + 2 * LANES], preferred_element_type=jnp.float32
            )
            if group < groups - 1:
                begin = (group + 1) * some
                taper(group + 1, range(begin + tile * some // tiles, begin + (tile + 1) * some // tiles))
            real = jnp.zeros((some, LANES), jnp.float32)
            imag = jnp.zeros((some, LANES), jnp.float32)
            for r in range(rows):
                part = product[r * some : (r + 1) * some, :]
                twist_re = waves[0, twist_row + r : twist_row + r + 1, cut]
                twist_im = -waves[1, twist_row + r : twist_row + r + 1, cut]
                part_re, part_im = part[:, :LANES], part[:, LANES:]
                real = real + (part_re * twist_re - part_im * twist_im)
                imag = imag + (part_re * twist_im + part_im * twist_re)
            spectra.append((real, imag))
            powers.append(real * real + imag * imag)
            if tile:
                whiten(group, spectra, powers, windows, tile - 1)
            elif group == groups - 1:
                write_energy()
        whiten(group, spectra, powers, windows, tiles - 1)


def transform(strain, offsets, bins):
    count, width = offsets.shape[0], bins.shape[0]
    samples = strain.shape[1]
    rows = -(-(SEGLEN + LANES - 1) // (8 * DEPTH)) * 8
    groups = GROUPS if count % (16 * GROUPS) == 0 else 1
    lines = -(-(samples // LANES + DEPTH // LANES) // 8) * 8
    vmem = pl.BlockSpec(memory_space=pltpu.VMEM)
    hbm = pl.BlockSpec(memory_space=pltpu.HBM)
    return pl.pallas_call(
        functools.partial(transform_kernel, count, groups, rows, width),
        out_shape=jax.ShapeDtypeStruct((2 * width // LANES * count + EXTRA, LANES), jnp.bfloat16),
        in_specs=[hbm] * 3,
        out_specs=vmem,
        scratch_shapes=[
            pltpu.SMEM(offsets.shape, jnp.int32),
            pltpu.VMEM(strain.shape, strain.dtype),
            pltpu.VMEM(bins.shape, jnp.int32),
            pltpu.VMEM((2, rows, DEPTH), jnp.float32),
            pltpu.VMEM((1, width), jnp.float32),
            pltpu.VMEM((lines, LANES), jnp.float32),
            pltpu.VMEM((3, count, LANES), jnp.float32),
            pltpu.VMEM((groups, DEPTH // LANES, rows * count // groups, LANES), jnp.float32),
            pltpu.VMEM((count, LANES), jnp.float32),
            pltpu.VMEM((DEPTH, 2 * width), jnp.bfloat16),
            pltpu.VMEM((2, EDGE + DEPTH // EDGE + rows, width), jnp.float32),
            pltpu.SemaphoreType.DMA((3,)),
        ],
        compiler_params=pltpu.CompilerParams(vmem_limit_bytes=VMEM_LIMIT),
        cost_estimate=pl.CostEstimate(flops=400 << 20, bytes_accessed=6 << 20, transcendentals=0),
        name="transform",
    )(offsets, strain, bins)


def energy_of(payload):
    return jnp.sum(payload[-EXTRA:, :].astype(jnp.float32), axis=0, keepdims=True)


def weights_of(energy, count, channels):
    lane = lax.broadcasted_iota(jnp.int32, (count, LANES), 1)
    line = lax.broadcasted_iota(jnp.int32, (count, LANES), 0)
    weight = 1.0 / (energy * (1.0 / (channels * SEGLEN)) + EPS)
    weight = jnp.where(lane[0:1] < count, weight, 0.0)
    scale = 1.0 / jnp.sum(weight, axis=1, keepdims=True)
    column = jnp.sum(jnp.where(lane == line, weight, 0.0), axis=1, keepdims=True)
    return jnp.broadcast_to(column, (count, LANES)), scale


AXES = ("x", "c", "z", "y")


def places_here():
    x_size, c_size, z_size, y_size = (lax.axis_size(a) for a in AXES)
    x, c, z, y = (lax.axis_index(a) for a in AXES)
    across = [f(x) * c_size + g(c) for g in partners(c_size) for f in partners(x_size)]
    up = [f(z) * y_size + y for f in partners(z_size)]
    up = up + [z * y_size + g(y) for g in partners(y_size)[1:]]
    up = up + [f(z) * y_size + g(y) for f in partners(z_size)[1:] for g in partners(y_size)[1:]]
    return up, across


def cross_kernel(left_count, right_count, count, channels, energy, *refs):
    left, right = refs[:left_count], refs[left_count : left_count + right_count]
    out, block, sems = refs[left_count + right_count :]
    weight, scale = weights_of(energy[...], count, channels)
    share = weight * scale
    up, across = places_here()
    copies = []
    for tile in range(block.shape[-1] // LANES):
        cut = slice(tile * LANES, (tile + 1) * LANES)
        at_re = slice(2 * tile * count, (2 * tile + 1) * count)
        at_im = slice((2 * tile + 1) * count, (2 * tile + 2) * count)
        rights = [
            (ref[at_re, :].astype(jnp.float32), ref[at_im, :].astype(jnp.float32)) for ref in right
        ]
        for i, ref in enumerate(left):
            left_re = ref[at_re, :].astype(jnp.float32) * share
            left_im = ref[at_im, :].astype(jnp.float32) * share
            for j, (right_re, right_im) in enumerate(rights):
                real = left_re * right_re + left_im * right_im
                imag = left_im * right_re - left_re * right_im
                at = up[i], across[j]
                block[at[0], at[1], 0, 0:1, cut] = jnp.sum(real, axis=0, keepdims=True)
                block[at[0], at[1], 0, 1:2, cut] = jnp.sum(imag, axis=0, keepdims=True)
        part = (slice(None),) * 4 + (cut,)
        copies.append(pltpu.make_async_copy(block.at[part], out.at[part], sems.at[tile]))
        copies[-1].start()
    for copy in copies:
        copy.wait()


def cross(energy, left, right, count, width, channels):
    vmem = pl.BlockSpec(memory_space=pltpu.VMEM)
    arrays = [energy, *left, *right]
    return pl.pallas_call(
        functools.partial(cross_kernel, len(left), len(right), count, channels),
        out_shape=jax.ShapeDtypeStruct((len(left), len(right), 1, 2, width), jnp.float32),
        in_specs=[vmem] * len(arrays),
        out_specs=pl.BlockSpec(memory_space=pltpu.HBM),
        scratch_shapes=[
            pltpu.VMEM((len(left), len(right), 1, 2, width), jnp.float32),
            pltpu.SemaphoreType.DMA((width // LANES,)),
        ],
        compiler_params=pltpu.CompilerParams(vmem_limit_bytes=CROSS_VMEM),
        cost_estimate=pl.CostEstimate(flops=4 << 20, bytes_accessed=2 << 20, transcendentals=0),
        name="cross",
    )(*arrays)


def product_kernel(left_count, right_count, count, *refs):
    left, right = refs[:left_count], refs[left_count : left_count + right_count]
    products = refs[-1]
    for tile in range(products.shape[1] // 2):
        at_re = slice(2 * tile * count, (2 * tile + 1) * count)
        at_im = slice((2 * tile + 1) * count, (2 * tile + 2) * count)
        rights = [
            (ref[at_re, :].astype(jnp.float32), ref[at_im, :].astype(jnp.float32)) for ref in right
        ]
        for i, ref in enumerate(left):
            left_re = ref[at_re, :].astype(jnp.float32)
            left_im = ref[at_im, :].astype(jnp.float32)
            for j, (right_re, right_im) in enumerate(rights):
                pair = i * right_count + j
                products[pair, 2 * tile] = left_re * right_re + left_im * right_im
                products[pair, 2 * tile + 1] = left_im * right_re - left_re * right_im


def pair_products(left, right, count, width):
    pairs = len(left) * len(right)
    vmem = pl.BlockSpec(memory_space=pltpu.VMEM)
    return pl.pallas_call(
        functools.partial(product_kernel, len(left), len(right), count),
        out_shape=jax.ShapeDtypeStruct((pairs, 2 * width // LANES, count, LANES), jnp.float32),
        in_specs=[vmem] * (len(left) + len(right)),
        out_specs=vmem,
        compiler_params=pltpu.CompilerParams(vmem_limit_bytes=CROSS_VMEM),
        cost_estimate=pl.CostEstimate(flops=4 << 20, bytes_accessed=2 << 20, transcendentals=0),
        name="pair_products",
    )(*left, *right)


def sublane_sums(values):
    row = lax.broadcasted_iota(jnp.int32, (8, LANES), 0)
    for bit in (4, 2, 1):
        low = (row & bit) == 0
        packed = []
        for q in range(bit):
            a, b = values[q], values[q + bit]
            theirs = jnp.where(low, b, a)
            down = pltpu.roll(theirs, bit, 0)
            if bit < 4:
                down = jnp.where(low, pltpu.roll(theirs, 8 - bit, 0), down)
            packed.append(jnp.where(low, a, b) + down)
        values = packed
    return values[0]


def stack_kernel(left_count, right_count, channels, energy, products, out, block, sems):
    count = products.shape[2]
    weight, scale = weights_of(energy[...], count, channels)
    up, across = places_here()
    copies = []
    for tile in range(block.shape[-1] // LANES):
        cut = slice(tile * LANES, (tile + 1) * LANES)
        for i in range(left_count):
            at = up[i]
            for first in range(0, right_count, 4):
                some = range(first, min(first + 4, right_count))
                sums = []
                for j in some:
                    for part in range(2):
                        total = jnp.zeros((8, LANES), jnp.float32)
                        for begin in range(0, count, 8):
                            here = slice(begin, begin + 8)
                            product = products[i * right_count + j, 2 * tile + part, here, :]
                            total = total + product * weight[here, :]
                        sums.append(total)
                sums = sublane_sums(sums + [sums[0]] * (8 - len(sums))) * scale
                for k, j in enumerate(some):
                    block[at, across[j], 0, :, cut] = sums[2 * k : 2 * k + 2, :]
        part = (slice(None),) * 4 + (cut,)
        copies.append(pltpu.make_async_copy(block.at[part], out.at[part], sems.at[tile]))
        copies[-1].start()
    for copy in copies:
        copy.wait()


def stack(energy, products, left_count, right_count, width, channels):
    vmem = pl.BlockSpec(memory_space=pltpu.VMEM)
    shape = (left_count, right_count, 1, 2, width)
    return pl.pallas_call(
        functools.partial(stack_kernel, left_count, right_count, channels),
        out_shape=jax.ShapeDtypeStruct(shape, jnp.float32),
        in_specs=[vmem, vmem],
        out_specs=pl.BlockSpec(memory_space=pltpu.HBM),
        scratch_shapes=[
            pltpu.VMEM(shape, jnp.float32),
            pltpu.SemaphoreType.DMA((width // LANES,)),
        ],
        compiler_params=pltpu.CompilerParams(vmem_limit_bytes=CROSS_VMEM),
        cost_estimate=pl.CostEstimate(flops=4 << 20, bytes_accessed=2 << 20, transcendentals=0),
        name="stack",
    )(energy, products)


def partners(size):
    if size & (size - 1) == 0:
        return [lambda p, k=k: p ^ k for k in range(size)]
    return [lambda p, k=k: (p - k) % size for k in range(size)]


def fetch(x, axis, size, step):
    source = partners(size)[step]
    return lax.ppermute(x, axis, [(source(p), p) for p in range(size)])


def fetch_all(x, axis, size):
    return [fetch(x, axis, size, step) for step in range(size - 1, 0, -1)][::-1]


def per_device(row_size, col_size, strain, offsets, bins):
    x_size, c_size, z_size, y_size = (lax.axis_size(a) for a in AXES)
    channels = row_size * col_size
    own = transform(strain, offsets, bins)

    column = [own] + fetch_all(own, "z", z_size)
    beside = fetch_all(own, "x", x_size)
    other = fetch_all(own, "y", y_size)
    soon = [fetch(w, "y", y_size, step) for w in column[3:] for step in range(1, y_size)]
    kept = own.astype(jnp.float32)
    other, beside, soon, column, kept = lax.optimization_barrier((other, beside, soon, column, kept))
    near = functools.reduce(jnp.add, [energy_of(w) for w in column[1:]], energy_of(kept))

    forward = [fetch(w, "y", y_size, step) for w in column[1:3] for step in range(1, y_size)]
    far = []
    for i in range(1, x_size):
        for j in range(y_size):
            pairs = [
                (partners(x_size)[i](x) * y_size + partners(y_size)[j](y), x * y_size + y)
                for x in range(x_size)
                for y in range(y_size)
            ]
            far.append(lax.ppermute(near, ("x", "y"), pairs))
    forward, far, near = lax.optimization_barrier((forward, far, near))
    forward = forward + soon
    energy = functools.reduce(jnp.add, [energy_of(w) for w in other + forward], near)
    energy = functools.reduce(jnp.add, far, energy)

    right = [kept] + beside
    right = right + [fetch(w, "c", c_size, step) for step in range(1, c_size) for w in [own] + beside]
    energy, right = lax.optimization_barrier((energy, right))
    energy = functools.reduce(jnp.add, fetch_all(energy, "c", c_size), energy)
    left = [kept] + column[1:] + other + forward
    count, width = offsets.shape[0], bins.shape[0]
    if len(left) * len(right) * count * 2 * width * 4 > PRODUCT_BYTES:
        return cross(energy, left, right, count, width, channels)
    products = pair_products(left, right, count, width)
    return stack(energy, products, len(left), len(right), width, channels)


def factors(size):
    return (size // 2, 2) if size % 2 == 0 else (size, 1)


def solution(mesh):
    row_size, col_size = mesh.shape["row"], mesh.shape["col"]
    shape = factors(row_size) + factors(col_size)
    fine = Mesh(mesh.devices.reshape(shape), AXES)
    return jax.shard_map(
        functools.partial(per_device, row_size, col_size),
        mesh=fine,
        in_specs=(P(("x", "c", "z", "y"), None), P(), P()),
        out_specs=P(("x", "c"), None, ("z", "y"), None, None),
        check_vma=False,
    )
```

```python
import functools
import math

import jax
import jax.numpy as jnp
from jax import lax
from jax.experimental import pallas as pl
from jax.experimental.pallas import tpu as pltpu
from jax.sharding import Mesh
from jax.sharding import PartitionSpec as P

SEGLEN = 6000
TAPER = 32
SMOOTH = 64
EPS = 1e-06
LANES = 128
DEPTH = 256
VMEM_LIMIT = 58 << 20
CROSS_VMEM = 16 << 20
PRODUCT_BYTES = 8 << 20
EXTRA = 16
PIECES = 3
GROUPS = 2
EDGE = 16


def turns_of(place):
    return place.astype(jnp.float32) * (2.0 * math.pi / SEGLEN)


def transform_kernel(
    count, groups, rows, width, offsets_hbm, strain_hbm, bins_hbm, payload,
    offsets, strain, bins, trig, ramp, record, shift, blocks, sums, table, waves, sems,
):
    arrivals = [
        pltpu.make_async_copy(source, target, sems.at[i])
        for i, (source, target) in enumerate(
            [(bins_hbm, bins), (offsets_hbm, offsets), (strain_hbm, strain)]
        )
    ]
    for copy in arrivals:
        copy.start()

    line = lax.broadcasted_iota(jnp.int32, (rows, DEPTH), 0)
    turn = turns_of(line * DEPTH + lax.broadcasted_iota(jnp.int32, (rows, DEPTH), 1))
    trig[0] = 0.5 * jnp.cos(turn)
    trig[1] = 0.5 * jnp.sin(turn)
    bin_at = lax.broadcasted_iota(jnp.int32, (1, width), 1).astype(jnp.float32) + 0.5
    rise = jnp.minimum(jnp.minimum(bin_at, width - bin_at) * (1.0 / TAPER), 1.0)
    ramp[...] = jnp.square(jnp.sin(0.5 * math.pi * rise))

    arrivals[0].wait()
    high_rows = DEPTH // EDGE
    twist_row = EDGE + high_rows
    mult_row = lax.broadcasted_iota(jnp.int32, (twist_row + rows, 1), 0)
    mult = jnp.where(
        mult_row < EDGE,
        mult_row,
        jnp.where(mult_row < twist_row, (mult_row - EDGE) * EDGE, (mult_row - twist_row) * DEPTH),
    ).astype(jnp.float32)
    phase = mult * bins[...].reshape(1, width).astype(jnp.float32)
    turns = jnp.floor(phase * (1.0 / SEGLEN) + 0.5)
    angle = turns_of(phase - turns * SEGLEN)
    waves[0] = jnp.cos(angle)
    waves[1] = jnp.sin(angle)
    tiles = width // LANES
    low_cos = waves[0, 0:EDGE, :]
    low_sin = waves[1, 0:EDGE, :]
    for high in range(high_rows):
        at = EDGE + high
        high_cos = waves[0, at : at + 1, :]
        high_sin = waves[1, at : at + 1, :]
        real = high_cos * low_cos - high_sin * low_sin
        imag = -(high_sin * low_cos + high_cos * low_sin)
        for tile in range(tiles):
            cut = slice(tile * LANES, (tile + 1) * LANES)
            to = 2 * tile * LANES
            here = slice(high * EDGE, (high + 1) * EDGE)
            table[here, to : to + LANES] = real[:, cut].astype(jnp.bfloat16)
            table[here, to + LANES : to + 2 * LANES] = imag[:, cut].astype(jnp.bfloat16)
    arrivals[1].wait()
    for s in range(count):
        inside = (offsets[s] & (LANES - 1)).astype(jnp.float32)
        shift[0, s : s + 1, :] = jnp.full((1, LANES), inside, jnp.float32)
    turn = turns_of(shift[0])
    shift[1] = jnp.cos(turn)
    shift[2] = jnp.sin(turn)
    for copy in arrivals[2:]:
        copy.wait()
    samples = strain.shape[1]
    chunk = LANES * 8 * 8
    begin = 0
    while begin < samples:
        size = min(chunk, samples - begin)
        part = strain[:, begin : begin + size].astype(jnp.float32)
        record[begin // LANES : (begin + size) // LANES, :] = part.reshape(size // LANES, LANES)
        begin += size
    tail = record.shape[0] - samples // LANES
    record[samples // LANES :, :] = jnp.zeros((tail, LANES), jnp.float32)
    place = (
        lax.broadcasted_iota(jnp.int32, (8, LANES), 0) * DEPTH
        + lax.broadcasted_iota(jnp.int32, (8, LANES), 1)
    ).astype(jnp.float32)
    steps = DEPTH // LANES
    some = count // groups

    def taper(group, segments):
        for s in segments:
            first = offsets[s] // LANES
            moved = place - shift[0, s : s + 1, :]
            turn_cos = shift[1, s : s + 1, :]
            turn_sin = shift[2, s : s + 1, :]
            total = jnp.zeros((8, LANES), jnp.float32)
            for start in range(0, rows, 8):
                here = slice(start, start + 8)
                for part in range(steps):
                    lanes = slice(part * LANES, (part + 1) * LANES)
                    block = record[pl.ds(first + part + steps * start, 8, stride=steps), :]
                    window = 0.5 - (trig[0, here, lanes] * turn_cos + trig[1, here, lanes] * turn_sin)
                    value = block * window
                    sample = start * DEPTH + part * LANES
                    if sample == 0:
                        value = jnp.where(moved > -0.5, value, 0.0)
                    if (start + 7) * DEPTH + (part + 1) * LANES > SEGLEN:
                        value = jnp.where(moved < SEGLEN - sample - 0.5, value, 0.0)
                    value = value.astype(jnp.bfloat16).astype(jnp.float32)
                    total = total + value * value
                    at = s - group * some + start * some
                    blocks[group, part, pl.ds(at, 8, stride=some), :] = value
            sums[s : s + 1, :] = jnp.sum(total, axis=0, keepdims=True)

    def tapered_group(group):
        return jnp.concatenate(
            [blocks[group, part].astype(jnp.bfloat16) for part in range(steps)], axis=1
        )

    def window_sums(powers, tile):
        above = powers[min(tile + 1, tiles - 1)]
        sums = jnp.concatenate([powers[tile], above], axis=1)
        reach = 1
        while reach < SMOOTH:
            sums = sums + sum(pltpu.roll(sums, 2 * LANES - k * reach, 1) for k in range(1, 4))
            reach *= 4
        return pltpu.roll(sums[:, :LANES], SMOOTH // 2, 1)

    def whiten(group, spectra, powers, windows, tile):
        windows.append(window_sums(powers, tile))
        lane = lax.broadcasted_iota(jnp.int32, (some, LANES), 1)
        begin, end = SMOOTH // 2, LANES - SMOOTH // 2
        under = windows[tile][:, begin : begin + 1] if tile == 0 else windows[tile - 1]
        power = jnp.where(lane < begin, under, windows[tile])
        if tile == tiles - 1:
            power = jnp.where(lane > end, power[:, end : end + 1], power)
        cut = slice(tile * LANES, (tile + 1) * LANES)
        scale = ramp[:, cut] * lax.rsqrt(power * (1.0 / SMOOTH) + EPS)
        real, imag = spectra[tile]
        at = 2 * tile * count + group * some
        payload[at : at + some, :] = (real * scale).astype(jnp.bfloat16)
        payload[at + count : at + count + some, :] = (imag * scale).astype(jnp.bfloat16)

    def write_energy():
        lane = lax.broadcasted_iota(jnp.int32, (count, LANES), 1)
        line = lax.broadcasted_iota(jnp.int32, (count, LANES), 0)
        whole = jnp.sum(sums[...], axis=1, keepdims=True)
        rest = jnp.sum(jnp.where(lane == line, whole, 0.0), axis=0, keepdims=True)
        place = lax.broadcasted_iota(jnp.int32, (EXTRA, LANES), 0)
        extra = jnp.zeros((EXTRA, LANES), jnp.float32)
        for i in range(PIECES):
            piece = rest.astype(jnp.bfloat16).astype(jnp.float32)
            extra = jnp.where(place == i, piece, extra)
            rest = rest - piece
        payload[2 * tiles * count :, :] = extra.astype(jnp.bfloat16)
    taper(0, range(some))
    for group in range(groups):
        tapered = tapered_group(group)
        spectra, powers, windows = [], [], []
        for tile in range(tiles):
            cut = slice(tile * LANES, (tile + 1) * LANES)
            to = 2 * tile * LANES
            product = jnp.dot(
                tapered, table[:, to : to + 2 * LANES], preferred_element_type=jnp.float32
            )
            if group < groups - 1:
                begin = (group + 1) * some
                taper(group + 1, range(begin + tile * some // tiles, begin + (tile + 1) * some // tiles))
            real = jnp.zeros((some, LANES), jnp.float32)
            imag = jnp.zeros((some, LANES), jnp.float32)
            for r in range(rows):
                part = product[r * some : (r + 1) * some, :]
                twist_re = waves[0, twist_row + r : twist_row + r + 1, cut]
                twist_im = -waves[1, twist_row + r : twist_row + r + 1, cut]
                part_re, part_im = part[:, :LANES], part[:, LANES:]
                real = real + (part_re * twist_re - part_im * twist_im)
                imag = imag + (part_re * twist_im + part_im * twist_re)
            spectra.append((real, imag))
            powers.append(real * real + imag * imag)
            if tile:
                whiten(group, spectra, powers, windows, tile - 1)
            elif group == groups - 1:
                write_energy()
        whiten(group, spectra, powers, windows, tiles - 1)


def transform(strain, offsets, bins):
    count, width = offsets.shape[0], bins.shape[0]
    samples = strain.shape[1]
    rows = -(-(SEGLEN + LANES - 1) // (8 * DEPTH)) * 8
    groups = GROUPS if count % (16 * GROUPS) == 0 else 1
    lines = -(-(samples // LANES + DEPTH // LANES) // 8) * 8
    vmem = pl.BlockSpec(memory_space=pltpu.VMEM)
    hbm = pl.BlockSpec(memory_space=pltpu.HBM)
    return pl.pallas_call(
        functools.partial(transform_kernel, count, groups, rows, width),
        out_shape=jax.ShapeDtypeStruct((2 * width // LANES * count + EXTRA, LANES), jnp.bfloat16),
        in_specs=[hbm] * 3,
        out_specs=vmem,
        scratch_shapes=[
            pltpu.SMEM(offsets.shape, jnp.int32),
            pltpu.VMEM(strain.shape, strain.dtype),
            pltpu.VMEM(bins.shape, jnp.int32),
            pltpu.VMEM((2, rows, DEPTH), jnp.float32),
            pltpu.VMEM((1, width), jnp.float32),
            pltpu.VMEM((lines, LANES), jnp.float32),
            pltpu.VMEM((3, count, LANES), jnp.float32),
            pltpu.VMEM((groups, DEPTH // LANES, rows * count // groups, LANES), jnp.float32),
            pltpu.VMEM((count, LANES), jnp.float32),
            pltpu.VMEM((DEPTH, 2 * width), jnp.bfloat16),
            pltpu.VMEM((2, EDGE + DEPTH // EDGE + rows, width), jnp.float32),
            pltpu.SemaphoreType.DMA((3,)),
        ],
        compiler_params=pltpu.CompilerParams(vmem_limit_bytes=VMEM_LIMIT),
        cost_estimate=pl.CostEstimate(flops=400 << 20, bytes_accessed=6 << 20, transcendentals=0),
        name="transform",
    )(offsets, strain, bins)


def energy_of(payload):
    return jnp.sum(payload[-EXTRA:, :].astype(jnp.float32), axis=0, keepdims=True)


def weights_of(energy, count, channels):
    lane = lax.broadcasted_iota(jnp.int32, (count, LANES), 1)
    line = lax.broadcasted_iota(jnp.int32, (count, LANES), 0)
    weight = 1.0 / (energy * (1.0 / (channels * SEGLEN)) + EPS)
    weight = jnp.where(lane[0:1] < count, weight, 0.0)
    scale = 1.0 / jnp.sum(weight, axis=1, keepdims=True)
    column = jnp.sum(jnp.where(lane == line, weight, 0.0), axis=1, keepdims=True)
    return jnp.broadcast_to(column, (count, LANES)), scale


AXES = ("x", "c", "z", "y")


def places_here():
    x_size, c_size, z_size, y_size = (lax.axis_size(a) for a in AXES)
    x, c, z, y = (lax.axis_index(a) for a in AXES)
    across = [f(x) * c_size + g(c) for g in partners(c_size) for f in partners(x_size)]
    up = [f(z) * y_size + y for f in partners(z_size)]
    up = up + [z * y_size + g(y) for g in partners(y_size)[1:]]
    up = up + [f(z) * y_size + g(y) for f in partners(z_size)[1:] for g in partners(y_size)[1:]]
    return up, across


def cross_kernel(left_count, right_count, count, channels, energy, *refs):
    left, right = refs[:left_count], refs[left_count : left_count + right_count]
    out, block, sems = refs[left_count + right_count :]
    weight, scale = weights_of(energy[...], count, channels)
    share = weight * scale
    up, across = places_here()
    copies = []
    for tile in range(block.shape[-1] // LANES):
        cut = slice(tile * LANES, (tile + 1) * LANES)
        at_re = slice(2 * tile * count, (2 * tile + 1) * count)
        at_im = slice((2 * tile + 1) * count, (2 * tile + 2) * count)
        rights = [
            (ref[at_re, :].astype(jnp.float32), ref[at_im, :].astype(jnp.float32)) for ref in right
        ]
        for i, ref in enumerate(left):
            left_re = ref[at_re, :].astype(jnp.float32) * share
            left_im = ref[at_im, :].astype(jnp.float32) * share
            for j, (right_re, right_im) in enumerate(rights):
                real = left_re * right_re + left_im * right_im
                imag = left_im * right_re - left_re * right_im
                at = up[i], across[j]
                block[at[0], at[1], 0, 0:1, cut] = jnp.sum(real, axis=0, keepdims=True)
                block[at[0], at[1], 0, 1:2, cut] = jnp.sum(imag, axis=0, keepdims=True)
        part = (slice(None),) * 4 + (cut,)
        copies.append(pltpu.make_async_copy(block.at[part], out.at[part], sems.at[tile]))
        copies[-1].start()
    for copy in copies:
        copy.wait()


def cross(energy, left, right, count, width, channels):
    vmem = pl.BlockSpec(memory_space=pltpu.VMEM)
    arrays = [energy, *left, *right]
    return pl.pallas_call(
        functools.partial(cross_kernel, len(left), len(right), count, channels),
        out_shape=jax.ShapeDtypeStruct((len(left), len(right), 1, 2, width), jnp.float32),
        in_specs=[vmem] * len(arrays),
        out_specs=pl.BlockSpec(memory_space=pltpu.HBM),
        scratch_shapes=[
            pltpu.VMEM((len(left), len(right), 1, 2, width), jnp.float32),
            pltpu.SemaphoreType.DMA((width // LANES,)),
        ],
        compiler_params=pltpu.CompilerParams(vmem_limit_bytes=CROSS_VMEM),
        cost_estimate=pl.CostEstimate(flops=4 << 20, bytes_accessed=2 << 20, transcendentals=0),
        name="cross",
    )(*arrays)


def product_kernel(left_count, right_count, count, *refs):
    left, right = refs[:left_count], refs[left_count : left_count + right_count]
    products = refs[-1]
    for tile in range(products.shape[1] // 2):
        at_re = slice(2 * tile * count, (2 * tile + 1) * count)
        at_im = slice((2 * tile + 1) * count, (2 * tile + 2) * count)
        rights = [
            (ref[at_re, :].astype(jnp.float32), ref[at_im, :].astype(jnp.float32)) for ref in right
        ]
        for i, ref in enumerate(left):
            left_re = ref[at_re, :].astype(jnp.float32)
            left_im = ref[at_im, :].astype(jnp.float32)
            for j, (right_re, right_im) in enumerate(rights):
                pair = i * right_count + j
                products[pair, 2 * tile] = left_re * right_re + left_im * right_im
                products[pair, 2 * tile + 1] = left_im * right_re - left_re * right_im


def pair_products(left, right, count, width):
    pairs = len(left) * len(right)
    vmem = pl.BlockSpec(memory_space=pltpu.VMEM)
    return pl.pallas_call(
        functools.partial(product_kernel, len(left), len(right), count),
        out_shape=jax.ShapeDtypeStruct((pairs, 2 * width // LANES, count, LANES), jnp.float32),
        in_specs=[vmem] * (len(left) + len(right)),
        out_specs=vmem,
        compiler_params=pltpu.CompilerParams(vmem_limit_bytes=CROSS_VMEM),
        cost_estimate=pl.CostEstimate(flops=4 << 20, bytes_accessed=2 << 20, transcendentals=0),
        name="pair_products",
    )(*left, *right)


def sublane_sums(values):
    row = lax.broadcasted_iota(jnp.int32, (8, LANES), 0)
    for bit in (4, 2, 1):
        low = (row & bit) == 0
        packed = []
        for q in range(bit):
            a, b = values[q], values[q + bit]
            theirs = jnp.where(low, b, a)
            down = pltpu.roll(theirs, bit, 0)
            if bit < 4:
                down = jnp.where(low, pltpu.roll(theirs, 8 - bit, 0), down)
            packed.append(jnp.where(low, a, b) + down)
        values = packed
    return values[0]


def stack_kernel(left_count, right_count, channels, energy, products, out, block, sems):
    count = products.shape[2]
    weight, scale = weights_of(energy[...], count, channels)
    up, across = places_here()
    copies = []
    for tile in range(block.shape[-1] // LANES):
        cut = slice(tile * LANES, (tile + 1) * LANES)
        for i in range(left_count):
            at = up[i]
            for first in range(0, right_count, 4):
                some = range(first, min(first + 4, right_count))
                sums = []
                for j in some:
                    for part in range(2):
                        total = jnp.zeros((8, LANES), jnp.float32)
                        for begin in range(0, count, 8):
                            here = slice(begin, begin + 8)
                            product = products[i * right_count + j, 2 * tile + part, here, :]
                            total = total + product * weight[here, :]
                        sums.append(total)
                sums = sublane_sums(sums + [sums[0]] * (8 - len(sums))) * scale
                for k, j in enumerate(some):
                    block[at, across[j], 0, :, cut] = sums[2 * k : 2 * k + 2, :]
        part = (slice(None),) * 4 + (cut,)
        copies.append(pltpu.make_async_copy(block.at[part], out.at[part], sems.at[tile]))
        copies[-1].start()
    for copy in copies:
        copy.wait()


def stack(energy, products, left_count, right_count, width, channels):
    vmem = pl.BlockSpec(memory_space=pltpu.VMEM)
    shape = (left_count, right_count, 1, 2, width)
    return pl.pallas_call(
        functools.partial(stack_kernel, left_count, right_count, channels),
        out_shape=jax.ShapeDtypeStruct(shape, jnp.float32),
        in_specs=[vmem, vmem],
        out_specs=pl.BlockSpec(memory_space=pltpu.HBM),
        scratch_shapes=[
            pltpu.VMEM(shape, jnp.float32),
            pltpu.SemaphoreType.DMA((width // LANES,)),
        ],
        compiler_params=pltpu.CompilerParams(vmem_limit_bytes=CROSS_VMEM),
        cost_estimate=pl.CostEstimate(flops=4 << 20, bytes_accessed=2 << 20, transcendentals=0),
        name="stack",
    )(energy, products)


def partners(size):
    if size & (size - 1) == 0:
        return [lambda p, k=k: p ^ k for k in range(size)]
    return [lambda p, k=k: (p - k) % size for k in range(size)]


def fetch(x, axis, size, step):
    source = partners(size)[step]
    return lax.ppermute(x, axis, [(source(p), p) for p in range(size)])


def fetch_all(x, axis, size):
    return [fetch(x, axis, size, step) for step in range(size - 1, 0, -1)][::-1]


def per_device(row_size, col_size, strain, offsets, bins):
    x_size, c_size, z_size, y_size = (lax.axis_size(a) for a in AXES)
    channels = row_size * col_size
    own = transform(strain, offsets, bins)

    column = [own] + fetch_all(own, "z", z_size)
    beside = fetch_all(own, "x", x_size)
    other = fetch_all(own, "y", y_size)
    forward = [fetch(w, "y", y_size, step) for w in column[1:] for step in range(1, y_size)]
    kept = own.astype(jnp.float32)
    other, forward, beside, column, kept = lax.optimization_barrier((other, forward, beside, column, kept))
    column_energy = [energy_of(w) for w in [kept] + column[1:] + other + forward]
    energy = functools.reduce(jnp.add, column_energy)

    right = [kept] + beside
    right = right + [fetch(w, "c", c_size, step) for step in range(1, c_size) for w in [own] + beside]
    energy = functools.reduce(jnp.add, fetch_all(energy, "x", x_size), energy)
    energy, right = lax.optimization_barrier((energy, right))
    energy = functools.reduce(jnp.add, fetch_all(energy, "c", c_size), energy)
    left = [kept] + column[1:] + other + forward
    count, width = offsets.shape[0], bins.shape[0]
    if len(left) * len(right) * count * 2 * width * 4 > PRODUCT_BYTES:
        return cross(energy, left, right, count, width, channels)
    products = pair_products(left, right, count, width)
    return stack(energy, products, len(left), len(right), width, channels)


def factors(size):
    return (size // 2, 2) if size % 2 == 0 else (size, 1)


def solution(mesh):
    row_size, col_size = mesh.shape["row"], mesh.shape["col"]
    shape = factors(row_size) + factors(col_size)
    fine = Mesh(mesh.devices.reshape(shape), AXES)
    return jax.shard_map(
        functools.partial(per_device, row_size, col_size),
        mesh=fine,
        in_specs=(P(("x", "c", "z", "y"), None), P(), P()),
        out_specs=P(("x", "c"), None, ("z", "y"), None, None),
        check_vma=False,
    )
```

```python
import functools
import math

import jax
import jax.numpy as jnp
from jax import lax
from jax.experimental import pallas as pl
from jax.experimental.pallas import tpu as pltpu
from jax.sharding import Mesh
from jax.sharding import PartitionSpec as P

SEGLEN = 6000
TAPER = 32
SMOOTH = 64
EPS = 1e-06
LANES = 128
DEPTH = 256
VMEM_LIMIT = 58 << 20
CROSS_VMEM = 16 << 20
PRODUCT_BYTES = 8 << 20
EXTRA = 16
PIECES = 3
GROUPS = 2
EDGE = 16


def turns_of(place):
    return place.astype(jnp.float32) * (2.0 * math.pi / SEGLEN)


def transform_kernel(
    count, groups, rows, width, offsets_hbm, strain_hbm, bins_hbm, payload,
    offsets, strain, bins, trig, ramp, record, shift, blocks, sums, table, waves, sems,
):
    arrivals = [
        pltpu.make_async_copy(source, target, sems.at[i])
        for i, (source, target) in enumerate(
            [(bins_hbm, bins), (offsets_hbm, offsets), (strain_hbm, strain)]
        )
    ]
    for copy in arrivals:
        copy.start()

    line = lax.broadcasted_iota(jnp.int32, (rows, DEPTH), 0)
    turn = turns_of(line * DEPTH + lax.broadcasted_iota(jnp.int32, (rows, DEPTH), 1))
    trig[0] = 0.5 * jnp.cos(turn)
    trig[1] = 0.5 * jnp.sin(turn)
    bin_at = lax.broadcasted_iota(jnp.int32, (1, width), 1).astype(jnp.float32) + 0.5
    rise = jnp.minimum(jnp.minimum(bin_at, width - bin_at) * (1.0 / TAPER), 1.0)
    ramp[...] = jnp.square(jnp.sin(0.5 * math.pi * rise))

    arrivals[0].wait()
    high_rows = DEPTH // EDGE
    twist_row = EDGE + high_rows
    mult_row = lax.broadcasted_iota(jnp.int32, (twist_row + rows, 1), 0)
    mult = jnp.where(
        mult_row < EDGE,
        mult_row,
        jnp.where(mult_row < twist_row, (mult_row - EDGE) * EDGE, (mult_row - twist_row) * DEPTH),
    ).astype(jnp.float32)
    phase = mult * bins[...].reshape(1, width).astype(jnp.float32)
    turns = jnp.floor(phase * (1.0 / SEGLEN) + 0.5)
    angle = turns_of(phase - turns * SEGLEN)
    waves[0] = jnp.cos(angle)
    waves[1] = jnp.sin(angle)
    tiles = width // LANES
    low_cos = waves[0, 0:EDGE, :]
    low_sin = waves[1, 0:EDGE, :]
    for high in range(high_rows):
        at = EDGE + high
        high_cos = waves[0, at : at + 1, :]
        high_sin = waves[1, at : at + 1, :]
        real = high_cos * low_cos - high_sin * low_sin
        imag = -(high_sin * low_cos + high_cos * low_sin)
        for tile in range(tiles):
            cut = slice(tile * LANES, (tile + 1) * LANES)
            to = 2 * tile * LANES
            here = slice(high * EDGE, (high + 1) * EDGE)
            table[here, to : to + LANES] = real[:, cut].astype(jnp.bfloat16)
            table[here, to + LANES : to + 2 * LANES] = imag[:, cut].astype(jnp.bfloat16)
    arrivals[1].wait()
    for s in range(count):
        inside = (offsets[s] & (LANES - 1)).astype(jnp.float32)
        shift[0, s : s + 1, :] = jnp.full((1, LANES), inside, jnp.float32)
    turn = turns_of(shift[0])
    shift[1] = jnp.cos(turn)
    shift[2] = jnp.sin(turn)
    for copy in arrivals[2:]:
        copy.wait()
    samples = strain.shape[1]
    chunk = LANES * 8 * 8
    begin = 0
    while begin < samples:
        size = min(chunk, samples - begin)
        part = strain[:, begin : begin + size].astype(jnp.float32)
        record[begin // LANES : (begin + size) // LANES, :] = part.reshape(size // LANES, LANES)
        begin += size
    tail = record.shape[0] - samples // LANES
    record[samples // LANES :, :] = jnp.zeros((tail, LANES), jnp.float32)
    place = (
        lax.broadcasted_iota(jnp.int32, (8, LANES), 0) * DEPTH
        + lax.broadcasted_iota(jnp.int32, (8, LANES), 1)
    ).astype(jnp.float32)
    steps = DEPTH // LANES
    some = count // groups

    def taper(group, segments):
        for s in segments:
            first = offsets[s] // LANES
            moved = place - shift[0, s : s + 1, :]
            turn_cos = shift[1, s : s + 1, :]
            turn_sin = shift[2, s : s + 1, :]
            total = jnp.zeros((8, LANES), jnp.float32)
            for start in range(0, rows, 8):
                here = slice(start, start + 8)
                for part in range(steps):
                    lanes = slice(part * LANES, (part + 1) * LANES)
                    block = record[pl.ds(first + part + steps * start, 8, stride=steps), :]
                    window = 0.5 - (trig[0, here, lanes] * turn_cos + trig[1, here, lanes] * turn_sin)
                    value = block * window
                    sample = start * DEPTH + part * LANES
                    if sample == 0:
                        value = jnp.where(moved > -0.5, value, 0.0)
                    if (start + 7) * DEPTH + (part + 1) * LANES > SEGLEN:
                        value = jnp.where(moved < SEGLEN - sample - 0.5, value, 0.0)
                    value = value.astype(jnp.bfloat16).astype(jnp.float32)
                    total = total + value * value
                    at = s - group * some + start * some
                    blocks[group, part, pl.ds(at, 8, stride=some), :] = value
            sums[s : s + 1, :] = jnp.sum(total, axis=0, keepdims=True)

    def tapered_group(group):
        return jnp.concatenate(
            [blocks[group, part, : rows * some].astype(jnp.bfloat16) for part in range(steps)],
            axis=1,
        )

    def window_sums(powers, tile):
        above = powers[min(tile + 1, tiles - 1)]
        sums = jnp.concatenate([powers[tile], above], axis=1)
        reach = 1
        while reach < SMOOTH:
            sums = sums + sum(pltpu.roll(sums, 2 * LANES - k * reach, 1) for k in range(1, 4))
            reach *= 4
        return pltpu.roll(sums[:, :LANES], SMOOTH // 2, 1)

    def whiten(group, spectra, powers, windows, tile):
        windows.append(window_sums(powers, tile))
        lane = lax.broadcasted_iota(jnp.int32, (some, LANES), 1)
        begin, end = SMOOTH // 2, LANES - SMOOTH // 2
        under = windows[tile][:, begin : begin + 1] if tile == 0 else windows[tile - 1]
        power = jnp.where(lane < begin, under, windows[tile])
        if tile == tiles - 1:
            power = jnp.where(lane > end, power[:, end : end + 1], power)
        cut = slice(tile * LANES, (tile + 1) * LANES)
        scale = ramp[:, cut] * lax.rsqrt(power * (1.0 / SMOOTH) + EPS)
        real, imag = spectra[tile]
        at = 2 * tile * count + group * some
        payload[at : at + some, :] = (real * scale).astype(jnp.bfloat16)
        payload[at + count : at + count + some, :] = (imag * scale).astype(jnp.bfloat16)

    def write_energy():
        lane = lax.broadcasted_iota(jnp.int32, (count, LANES), 1)
        line = lax.broadcasted_iota(jnp.int32, (count, LANES), 0)
        whole = jnp.sum(sums[...], axis=1, keepdims=True)
        rest = jnp.sum(jnp.where(lane == line, whole, 0.0), axis=0, keepdims=True)
        place = lax.broadcasted_iota(jnp.int32, (EXTRA, LANES), 0)
        extra = jnp.zeros((EXTRA, LANES), jnp.float32)
        for i in range(PIECES):
            piece = rest.astype(jnp.bfloat16).astype(jnp.float32)
            extra = jnp.where(place == i, piece, extra)
            rest = rest - piece
        payload[2 * tiles * count :, :] = extra.astype(jnp.bfloat16)
    taper(0, range(some))
    for group in range(groups):
        tapered = tapered_group(group)
        spectra, powers, windows = [], [], []
        for tile in range(tiles):
            cut = slice(tile * LANES, (tile + 1) * LANES)
            to = 2 * tile * LANES
            product = jnp.dot(
                tapered, table[:, to : to + 2 * LANES], preferred_element_type=jnp.float32
            )
            if group < groups - 1:
                begin = (group + 1) * some
                taper(group + 1, range(begin + tile * some // tiles, begin + (tile + 1) * some // tiles))
            real = jnp.zeros((some, LANES), jnp.float32)
            imag = jnp.zeros((some, LANES), jnp.float32)
            for r in range(rows):
                part = product[r * some : (r + 1) * some, :]
                twist_re = waves[0, twist_row + r : twist_row + r + 1, cut]
                twist_im = -waves[1, twist_row + r : twist_row + r + 1, cut]
                part_re, part_im = part[:, :LANES], part[:, LANES:]
                real = real + (part_re * twist_re - part_im * twist_im)
                imag = imag + (part_re * twist_im + part_im * twist_re)
            spectra.append((real, imag))
            powers.append(real * real + imag * imag)
            if tile:
                whiten(group, spectra, powers, windows, tile - 1)
            elif group == groups - 1:
                write_energy()
        whiten(group, spectra, powers, windows, tiles - 1)


def transform(strain, offsets, bins):
    count, width = offsets.shape[0], bins.shape[0]
    samples = strain.shape[1]
    rows = -(-(SEGLEN + LANES - 1) // (8 * DEPTH)) * 8
    groups = GROUPS if count % (16 * GROUPS) == 0 else 1
    lines = -(-(samples // LANES + DEPTH // LANES) // 8) * 8
    vmem = pl.BlockSpec(memory_space=pltpu.VMEM)
    hbm = pl.BlockSpec(memory_space=pltpu.HBM)
    return pl.pallas_call(
        functools.partial(transform_kernel, count, groups, rows, width),
        out_shape=jax.ShapeDtypeStruct((2 * width // LANES * count + EXTRA, LANES), jnp.bfloat16),
        in_specs=[hbm] * 3,
        out_specs=vmem,
        scratch_shapes=[
            pltpu.SMEM(offsets.shape, jnp.int32),
            pltpu.VMEM(strain.shape, strain.dtype),
            pltpu.VMEM(bins.shape, jnp.int32),
            pltpu.VMEM((2, rows, DEPTH), jnp.float32),
            pltpu.VMEM((1, width), jnp.float32),
            pltpu.VMEM((lines, LANES), jnp.float32),
            pltpu.VMEM((3, count, LANES), jnp.float32),
            pltpu.VMEM((groups, DEPTH // LANES, (rows + 1) * count // groups, LANES), jnp.float32),
            pltpu.VMEM((count, LANES), jnp.float32),
            pltpu.VMEM((DEPTH, 2 * width), jnp.bfloat16),
            pltpu.VMEM((2, EDGE + DEPTH // EDGE + rows, width), jnp.float32),
            pltpu.SemaphoreType.DMA((3,)),
        ],
        compiler_params=pltpu.CompilerParams(vmem_limit_bytes=VMEM_LIMIT),
        cost_estimate=pl.CostEstimate(flops=400 << 20, bytes_accessed=6 << 20, transcendentals=0),
        name="transform",
    )(offsets, strain, bins)


def energy_of(payload):
    return jnp.sum(payload[-EXTRA:, :].astype(jnp.float32), axis=0, keepdims=True)


def weights_of(energy, count, channels):
    lane = lax.broadcasted_iota(jnp.int32, (count, LANES), 1)
    line = lax.broadcasted_iota(jnp.int32, (count, LANES), 0)
    weight = 1.0 / (energy * (1.0 / (channels * SEGLEN)) + EPS)
    weight = jnp.where(lane[0:1] < count, weight, 0.0)
    scale = 1.0 / jnp.sum(weight, axis=1, keepdims=True)
    column = jnp.sum(jnp.where(lane == line, weight, 0.0), axis=1, keepdims=True)
    return jnp.broadcast_to(column, (count, LANES)), scale


AXES = ("x", "c", "z", "y")


def places_here():
    x_size, c_size, z_size, y_size = (lax.axis_size(a) for a in AXES)
    x, c, z, y = (lax.axis_index(a) for a in AXES)
    across = [f(x) * c_size + g(c) for g in partners(c_size) for f in partners(x_size)]
    up = [f(z) * y_size + y for f in partners(z_size)]
    up = up + [z * y_size + g(y) for g in partners(y_size)[1:]]
    up = up + [f(z) * y_size + g(y) for f in partners(z_size)[1:] for g in partners(y_size)[1:]]
    return up, across


def cross_kernel(left_count, right_count, count, channels, energy, *refs):
    left, right = refs[:left_count], refs[left_count : left_count + right_count]
    out, block, sems = refs[left_count + right_count :]
    weight, scale = weights_of(energy[...], count, channels)
    share = weight * scale
    up, across = places_here()
    copies = []
    for tile in range(block.shape[-1] // LANES):
        cut = slice(tile * LANES, (tile + 1) * LANES)
        at_re = slice(2 * tile * count, (2 * tile + 1) * count)
        at_im = slice((2 * tile + 1) * count, (2 * tile + 2) * count)
        rights = [
            (ref[at_re, :].astype(jnp.float32), ref[at_im, :].astype(jnp.float32)) for ref in right
        ]
        for i, ref in enumerate(left):
            left_re = ref[at_re, :].astype(jnp.float32) * share
            left_im = ref[at_im, :].astype(jnp.float32) * share
            for j, (right_re, right_im) in enumerate(rights):
                real = left_re * right_re + left_im * right_im
                imag = left_im * right_re - left_re * right_im
                at = up[i], across[j]
                block[at[0], at[1], 0, 0:1, cut] = jnp.sum(real, axis=0, keepdims=True)
                block[at[0], at[1], 0, 1:2, cut] = jnp.sum(imag, axis=0, keepdims=True)
        part = (slice(None),) * 4 + (cut,)
        copies.append(pltpu.make_async_copy(block.at[part], out.at[part], sems.at[tile]))
        copies[-1].start()
    for copy in copies:
        copy.wait()


def cross(energy, left, right, count, width, channels):
    vmem = pl.BlockSpec(memory_space=pltpu.VMEM)
    arrays = [energy, *left, *right]
    return pl.pallas_call(
        functools.partial(cross_kernel, len(left), len(right), count, channels),
        out_shape=jax.ShapeDtypeStruct((len(left), len(right), 1, 2, width), jnp.float32),
        in_specs=[vmem] * len(arrays),
        out_specs=pl.BlockSpec(memory_space=pltpu.HBM),
        scratch_shapes=[
            pltpu.VMEM((len(left), len(right), 1, 2, width), jnp.float32),
            pltpu.SemaphoreType.DMA((width // LANES,)),
        ],
        compiler_params=pltpu.CompilerParams(vmem_limit_bytes=CROSS_VMEM),
        cost_estimate=pl.CostEstimate(flops=4 << 20, bytes_accessed=2 << 20, transcendentals=0),
        name="cross",
    )(*arrays)


def product_kernel(left_count, right_count, count, *refs):
    left, right = refs[:left_count], refs[left_count : left_count + right_count]
    products = refs[-1]
    for tile in range(products.shape[1] // 2):
        at_re = slice(2 * tile * count, (2 * tile + 1) * count)
        at_im = slice((2 * tile + 1) * count, (2 * tile + 2) * count)
        rights = [
            (ref[at_re, :].astype(jnp.float32), ref[at_im, :].astype(jnp.float32)) for ref in right
        ]
        for i, ref in enumerate(left):
            left_re = ref[at_re, :].astype(jnp.float32)
            left_im = ref[at_im, :].astype(jnp.float32)
            for j, (right_re, right_im) in enumerate(rights):
                pair = i * right_count + j
                products[pair, 2 * tile] = left_re * right_re + left_im * right_im
                products[pair, 2 * tile + 1] = left_im * right_re - left_re * right_im


def pair_products(left, right, count, width):
    pairs = len(left) * len(right)
    vmem = pl.BlockSpec(memory_space=pltpu.VMEM)
    return pl.pallas_call(
        functools.partial(product_kernel, len(left), len(right), count),
        out_shape=jax.ShapeDtypeStruct((pairs, 2 * width // LANES, count, LANES), jnp.float32),
        in_specs=[vmem] * (len(left) + len(right)),
        out_specs=vmem,
        compiler_params=pltpu.CompilerParams(vmem_limit_bytes=CROSS_VMEM),
        cost_estimate=pl.CostEstimate(flops=4 << 20, bytes_accessed=2 << 20, transcendentals=0),
        name="pair_products",
    )(*left, *right)


def sublane_sums(values):
    row = lax.broadcasted_iota(jnp.int32, (8, LANES), 0)
    for bit in (4, 2, 1):
        low = (row & bit) == 0
        packed = []
        for q in range(bit):
            a, b = values[q], values[q + bit]
            theirs = jnp.where(low, b, a)
            down = pltpu.roll(theirs, bit, 0)
            if bit < 4:
                down = jnp.where(low, pltpu.roll(theirs, 8 - bit, 0), down)
            packed.append(jnp.where(low, a, b) + down)
        values = packed
    return values[0]


def stack_kernel(left_count, right_count, channels, energy, products, out, block, sems):
    count = products.shape[2]
    weight, scale = weights_of(energy[...], count, channels)
    up, across = places_here()
    copies = []
    for tile in range(block.shape[-1] // LANES):
        cut = slice(tile * LANES, (tile + 1) * LANES)
        for i in range(left_count):
            at = up[i]
            for first in range(0, right_count, 4):
                some = range(first, min(first + 4, right_count))
                sums = []
                for j in some:
                    for part in range(2):
                        total = jnp.zeros((8, LANES), jnp.float32)
                        for begin in range(0, count, 8):
                            here = slice(begin, begin + 8)
                            product = products[i * right_count + j, 2 * tile + part, here, :]
                            total = total + product * weight[here, :]
                        sums.append(total)
                sums = sublane_sums(sums + [sums[0]] * (8 - len(sums))) * scale
                for k, j in enumerate(some):
                    block[at, across[j], 0, :, cut] = sums[2 * k : 2 * k + 2, :]
        part = (slice(None),) * 4 + (cut,)
        copies.append(pltpu.make_async_copy(block.at[part], out.at[part], sems.at[tile]))
        copies[-1].start()
    for copy in copies:
        copy.wait()


def stack(energy, products, left_count, right_count, width, channels):
    vmem = pl.BlockSpec(memory_space=pltpu.VMEM)
    shape = (left_count, right_count, 1, 2, width)
    return pl.pallas_call(
        functools.partial(stack_kernel, left_count, right_count, channels),
        out_shape=jax.ShapeDtypeStruct(shape, jnp.float32),
        in_specs=[vmem, vmem],
        out_specs=pl.BlockSpec(memory_space=pltpu.HBM),
        scratch_shapes=[
            pltpu.VMEM(shape, jnp.float32),
            pltpu.SemaphoreType.DMA((width // LANES,)),
        ],
        compiler_params=pltpu.CompilerParams(vmem_limit_bytes=CROSS_VMEM),
        cost_estimate=pl.CostEstimate(flops=4 << 20, bytes_accessed=2 << 20, transcendentals=0),
        name="stack",
    )(energy, products)


def partners(size):
    if size & (size - 1) == 0:
        return [lambda p, k=k: p ^ k for k in range(size)]
    return [lambda p, k=k: (p - k) % size for k in range(size)]


def fetch(x, axis, size, step):
    source = partners(size)[step]
    return lax.ppermute(x, axis, [(source(p), p) for p in range(size)])


def fetch_all(x, axis, size):
    return [fetch(x, axis, size, step) for step in range(size - 1, 0, -1)][::-1]


def per_device(row_size, col_size, strain, offsets, bins):
    x_size, c_size, z_size, y_size = (lax.axis_size(a) for a in AXES)
    channels = row_size * col_size
    own = transform(strain, offsets, bins)

    column = [own] + fetch_all(own, "z", z_size)
    beside = fetch_all(own, "x", x_size)
    other = fetch_all(own, "y", y_size)
    forward = [fetch(w, "y", y_size, step) for w in column[1:] for step in range(1, y_size)]
    kept = own.astype(jnp.float32)
    other, forward, beside, column, kept = lax.optimization_barrier((other, forward, beside, column, kept))
    column_energy = [energy_of(w) for w in [kept] + column[1:] + other + forward]
    energy = functools.reduce(jnp.add, column_energy)

    right = [kept] + beside
    right = right + [fetch(w, "c", c_size, step) for step in range(1, c_size) for w in [own] + beside]
    energy = functools.reduce(jnp.add, fetch_all(energy, "x", x_size), energy)
    energy, right = lax.optimization_barrier((energy, right))
    energy = functools.reduce(jnp.add, fetch_all(energy, "c", c_size), energy)
    left = [kept] + column[1:] + other + forward
    count, width = offsets.shape[0], bins.shape[0]
    if len(left) * len(right) * count * 2 * width * 4 > PRODUCT_BYTES:
        return cross(energy, left, right, count, width, channels)
    products = pair_products(left, right, count, width)
    return stack(energy, products, len(left), len(right), width, channels)


def factors(size):
    return (size // 2, 2) if size % 2 == 0 else (size, 1)


def solution(mesh):
    row_size, col_size = mesh.shape["row"], mesh.shape["col"]
    shape = factors(row_size) + factors(col_size)
    fine = Mesh(mesh.devices.reshape(shape), AXES)
    return jax.shard_map(
        functools.partial(per_device, row_size, col_size),
        mesh=fine,
        in_specs=(P(("x", "c", "z", "y"), None), P(), P()),
        out_specs=P(("x", "c"), None, ("z", "y"), None, None),
        check_vma=False,
    )
```

```python
import functools
import math

import jax
import jax.numpy as jnp
from jax import lax
from jax.experimental import pallas as pl
from jax.experimental.pallas import tpu as pltpu
from jax.sharding import Mesh
from jax.sharding import PartitionSpec as P

SEGLEN = 6000
TAPER = 32
SMOOTH = 64
EPS = 1e-06
LANES = 128
DEPTH = 256
VMEM_LIMIT = 58 << 20
CROSS_VMEM = 16 << 20
PRODUCT_BYTES = 8 << 20
EXTRA = 16
PIECES = 3
GROUPS = 2
EDGE = 16


def turns_of(place):
    return place.astype(jnp.float32) * (2.0 * math.pi / SEGLEN)


def transform_kernel(
    count, groups, rows, width, offsets_hbm, strain_hbm, bins_hbm, payload,
    offsets, strain, bins, trig, ramp, record, shift, blocks, sums, table, waves, sems,
):
    arrivals = [
        pltpu.make_async_copy(source, target, sems.at[i])
        for i, (source, target) in enumerate(
            [(bins_hbm, bins), (offsets_hbm, offsets), (strain_hbm, strain)]
        )
    ]
    for copy in arrivals:
        copy.start()

    line = lax.broadcasted_iota(jnp.int32, (rows, DEPTH), 0)
    turn = turns_of(line * DEPTH + lax.broadcasted_iota(jnp.int32, (rows, DEPTH), 1))
    trig[0] = 0.5 * jnp.cos(turn)
    trig[1] = 0.5 * jnp.sin(turn)
    bin_at = lax.broadcasted_iota(jnp.int32, (1, width), 1).astype(jnp.float32) + 0.5
    rise = jnp.minimum(jnp.minimum(bin_at, width - bin_at) * (1.0 / TAPER), 1.0)
    ramp[...] = jnp.square(jnp.sin(0.5 * math.pi * rise))

    arrivals[0].wait()
    high_rows = DEPTH // EDGE
    twist_row = EDGE + high_rows
    mult_row = lax.broadcasted_iota(jnp.int32, (twist_row + rows, 1), 0)
    mult = jnp.where(
        mult_row < EDGE,
        mult_row,
        jnp.where(mult_row < twist_row, (mult_row - EDGE) * EDGE, (mult_row - twist_row) * DEPTH),
    ).astype(jnp.float32)
    phase = mult * bins[...].reshape(1, width).astype(jnp.float32)
    turns = jnp.floor(phase * (1.0 / SEGLEN) + 0.5)
    angle = turns_of(phase - turns * SEGLEN)
    waves[0] = jnp.cos(angle)
    waves[1] = jnp.sin(angle)
    tiles = width // LANES
    low_cos = waves[0, 0:EDGE, :]
    low_sin = waves[1, 0:EDGE, :]
    for high in range(high_rows):
        at = EDGE + high
        high_cos = waves[0, at : at + 1, :]
        high_sin = waves[1, at : at + 1, :]
        real = high_cos * low_cos - high_sin * low_sin
        imag = -(high_sin * low_cos + high_cos * low_sin)
        for tile in range(tiles):
            cut = slice(tile * LANES, (tile + 1) * LANES)
            to = 2 * tile * LANES
            here = slice(high * EDGE, (high + 1) * EDGE)
            table[here, to : to + LANES] = real[:, cut].astype(jnp.bfloat16)
            table[here, to + LANES : to + 2 * LANES] = imag[:, cut].astype(jnp.bfloat16)
    arrivals[1].wait()
    for s in range(count):
        inside = (offsets[s] & (LANES - 1)).astype(jnp.float32)
        shift[0, s : s + 1, :] = jnp.full((1, LANES), inside, jnp.float32)
    turn = turns_of(shift[0])
    shift[1] = jnp.cos(turn)
    shift[2] = jnp.sin(turn)
    for copy in arrivals[2:]:
        copy.wait()
    samples = strain.shape[1]
    chunk = LANES * 8 * 8
    begin = 0
    while begin < samples:
        size = min(chunk, samples - begin)
        part = strain[:, begin : begin + size].astype(jnp.float32)
        record[begin // LANES : (begin + size) // LANES, :] = part.reshape(size // LANES, LANES)
        begin += size
    tail = record.shape[0] - samples // LANES
    record[samples // LANES :, :] = jnp.zeros((tail, LANES), jnp.float32)
    place = (
        lax.broadcasted_iota(jnp.int32, (8, LANES), 0) * DEPTH
        + lax.broadcasted_iota(jnp.int32, (8, LANES), 1)
    ).astype(jnp.float32)
    steps = DEPTH // LANES
    some = count // groups

    def taper(group, segments):
        for s in segments:
            first = offsets[s] // LANES
            moved = place - shift[0, s : s + 1, :]
            turn_cos = shift[1, s : s + 1, :]
            turn_sin = shift[2, s : s + 1, :]
            total = jnp.zeros((8, LANES), jnp.float32)
            for start in range(0, rows, 8):
                here = slice(start, start + 8)
                for part in range(steps):
                    lanes = slice(part * LANES, (part + 1) * LANES)
                    block = record[pl.ds(first + part + steps * start, 8, stride=steps), :]
                    window = 0.5 - (trig[0, here, lanes] * turn_cos + trig[1, here, lanes] * turn_sin)
                    value = block * window
                    sample = start * DEPTH + part * LANES
                    if sample == 0:
                        value = jnp.where(moved > -0.5, value, 0.0)
                    if (start + 7) * DEPTH + (part + 1) * LANES > SEGLEN:
                        value = jnp.where(moved < SEGLEN - sample - 0.5, value, 0.0)
                    value = value.astype(jnp.bfloat16).astype(jnp.float32)
                    total = total + value * value
                    at = s - group * some + start * some
                    blocks[group, part, pl.ds(at, 8, stride=some), :] = value
            sums[s : s + 1, :] = jnp.sum(total, axis=0, keepdims=True)

    def tapered_group(group):
        return jnp.concatenate(
            [blocks[group, part, : rows * some].astype(jnp.bfloat16) for part in range(steps)],
            axis=1,
        )

    def window_sums(powers, tile):
        above = powers[min(tile + 1, tiles - 1)]
        sums = jnp.concatenate([powers[tile], above], axis=1)
        reach = 1
        while reach < SMOOTH:
            sums = sums + sum(pltpu.roll(sums, 2 * LANES - k * reach, 1) for k in range(1, 4))
            reach *= 4
        return pltpu.roll(sums[:, :LANES], SMOOTH // 2, 1)

    def whiten(group, spectra, powers, windows, tile):
        windows.append(window_sums(powers, tile))
        lane = lax.broadcasted_iota(jnp.int32, (some, LANES), 1)
        begin, end = SMOOTH // 2, LANES - SMOOTH // 2
        under = windows[tile][:, begin : begin + 1] if tile == 0 else windows[tile - 1]
        power = jnp.where(lane < begin, under, windows[tile])
        if tile == tiles - 1:
            power = jnp.where(lane > end, power[:, end : end + 1], power)
        cut = slice(tile * LANES, (tile + 1) * LANES)
        scale = ramp[:, cut] * lax.rsqrt(power * (1.0 / SMOOTH) + EPS)
        real, imag = spectra[tile]
        at = 2 * tile * count + group * some
        payload[at : at + some, :] = (real * scale).astype(jnp.bfloat16)
        payload[at + count : at + count + some, :] = (imag * scale).astype(jnp.bfloat16)

    def write_energy():
        lane = lax.broadcasted_iota(jnp.int32, (count, LANES), 1)
        line = lax.broadcasted_iota(jnp.int32, (count, LANES), 0)
        whole = jnp.sum(sums[...], axis=1, keepdims=True)
        rest = jnp.sum(jnp.where(lane == line, whole, 0.0), axis=0, keepdims=True)
        place = lax.broadcasted_iota(jnp.int32, (EXTRA, LANES), 0)
        extra = jnp.zeros((EXTRA, LANES), jnp.float32)
        for i in range(PIECES):
            piece = rest.astype(jnp.bfloat16).astype(jnp.float32)
            extra = jnp.where(place == i, piece, extra)
            rest = rest - piece
        payload[2 * tiles * count :, :] = extra.astype(jnp.bfloat16)
    taper(0, range(some))
    for group in range(groups):
        tapered = tapered_group(group)
        spectra, powers, windows = [], [], []
        for tile in range(tiles):
            cut = slice(tile * LANES, (tile + 1) * LANES)
            to = 2 * tile * LANES
            product = jnp.dot(
                tapered, table[:, to : to + 2 * LANES], preferred_element_type=jnp.float32
            )
            if group < groups - 1:
                begin = (group + 1) * some
                taper(group + 1, range(begin + tile * some // tiles, begin + (tile + 1) * some // tiles))
            real = jnp.zeros((some, LANES), jnp.float32)
            imag = jnp.zeros((some, LANES), jnp.float32)
            for r in range(rows):
                part = product[r * some : (r + 1) * some, :]
                twist_re = waves[0, twist_row + r : twist_row + r + 1, cut]
                twist_im = -waves[1, twist_row + r : twist_row + r + 1, cut]
                part_re, part_im = part[:, :LANES], part[:, LANES:]
                real = real + (part_re * twist_re - part_im * twist_im)
                imag = imag + (part_re * twist_im + part_im * twist_re)
            spectra.append((real, imag))
            powers.append(real * real + imag * imag)
            if tile:
                whiten(group, spectra, powers, windows, tile - 1)
            elif group == groups - 1:
                write_energy()
        whiten(group, spectra, powers, windows, tiles - 1)


def transform(strain, offsets, bins):
    count, width = offsets.shape[0], bins.shape[0]
    samples = strain.shape[1]
    rows = -(-(SEGLEN + LANES - 1) // (8 * DEPTH)) * 8
    groups = GROUPS if count % (16 * GROUPS) == 0 else 1
    lines = -(-(samples // LANES + DEPTH // LANES) // 8) * 8
    vmem = pl.BlockSpec(memory_space=pltpu.VMEM)
    hbm = pl.BlockSpec(memory_space=pltpu.HBM)
    return pl.pallas_call(
        functools.partial(transform_kernel, count, groups, rows, width),
        out_shape=jax.ShapeDtypeStruct((2 * width // LANES * count + EXTRA, LANES), jnp.bfloat16),
        in_specs=[hbm] * 3,
        out_specs=vmem,
        scratch_shapes=[
            pltpu.SMEM(offsets.shape, jnp.int32),
            pltpu.VMEM(strain.shape, strain.dtype),
            pltpu.VMEM(bins.shape, jnp.int32),
            pltpu.VMEM((2, rows, DEPTH), jnp.float32),
            pltpu.VMEM((1, width), jnp.float32),
            pltpu.VMEM((lines, LANES), jnp.float32),
            pltpu.VMEM((3, count, LANES), jnp.float32),
            pltpu.VMEM((groups, DEPTH // LANES, (rows + 1) * count // groups, LANES), jnp.float32),
            pltpu.VMEM((count, LANES), jnp.float32),
            pltpu.VMEM((DEPTH, 2 * width), jnp.bfloat16),
            pltpu.VMEM((2, EDGE + DEPTH // EDGE + rows, width), jnp.float32),
            pltpu.SemaphoreType.DMA((3,)),
        ],
        compiler_params=pltpu.CompilerParams(vmem_limit_bytes=VMEM_LIMIT),
        cost_estimate=pl.CostEstimate(flops=400 << 20, bytes_accessed=6 << 20, transcendentals=0),
        name="transform",
    )(offsets, strain, bins)


def energy_of(payload):
    return jnp.sum(payload[-EXTRA:, :].astype(jnp.float32), axis=0, keepdims=True)


def weights_of(energy, count, channels):
    lane = lax.broadcasted_iota(jnp.int32, (count, LANES), 1)
    line = lax.broadcasted_iota(jnp.int32, (count, LANES), 0)
    weight = 1.0 / (energy * (1.0 / (channels * SEGLEN)) + EPS)
    weight = jnp.where(lane[0:1] < count, weight, 0.0)
    scale = 1.0 / jnp.sum(weight, axis=1, keepdims=True)
    column = jnp.sum(jnp.where(lane == line, weight, 0.0), axis=1, keepdims=True)
    return jnp.broadcast_to(column, (count, LANES)), scale


AXES = ("x", "c", "z", "y")


def places_here():
    x_size, c_size, z_size, y_size = (lax.axis_size(a) for a in AXES)
    x, c, z, y = (lax.axis_index(a) for a in AXES)
    across = [f(x) * c_size + g(c) for g in partners(c_size) for f in partners(x_size)]
    up = [f(z) * y_size + y for f in partners(z_size)]
    up = up + [z * y_size + g(y) for g in partners(y_size)[1:]]
    up = up + [f(z) * y_size + g(y) for f in partners(z_size)[1:] for g in partners(y_size)[1:]]
    return up, across


def cross_kernel(left_count, right_count, count, channels, energy, *refs):
    left, right = refs[:left_count], refs[left_count : left_count + right_count]
    out, block, sems = refs[left_count + right_count :]
    weight, scale = weights_of(energy[...], count, channels)
    share = weight * scale
    up, across = places_here()
    copies = []
    for tile in range(block.shape[-1] // LANES):
        cut = slice(tile * LANES, (tile + 1) * LANES)
        at_re = slice(2 * tile * count, (2 * tile + 1) * count)
        at_im = slice((2 * tile + 1) * count, (2 * tile + 2) * count)
        rights = [
            (ref[at_re, :].astype(jnp.float32), ref[at_im, :].astype(jnp.float32)) for ref in right
        ]
        for i, ref in enumerate(left):
            left_re = ref[at_re, :].astype(jnp.float32) * share
            left_im = ref[at_im, :].astype(jnp.float32) * share
            for j, (right_re, right_im) in enumerate(rights):
                real = left_re * right_re + left_im * right_im
                imag = left_im * right_re - left_re * right_im
                at = up[i], across[j]
                block[at[0], at[1], 0, 0:1, cut] = jnp.sum(real, axis=0, keepdims=True)
                block[at[0], at[1], 0, 1:2, cut] = jnp.sum(imag, axis=0, keepdims=True)
        part = (slice(None),) * 4 + (cut,)
        copies.append(pltpu.make_async_copy(block.at[part], out.at[part], sems.at[tile]))
        copies[-1].start()
    for copy in copies:
        copy.wait()


def cross(energy, left, right, count, width, channels):
    vmem = pl.BlockSpec(memory_space=pltpu.VMEM)
    arrays = [energy, *left, *right]
    return pl.pallas_call(
        functools.partial(cross_kernel, len(left), len(right), count, channels),
        out_shape=jax.ShapeDtypeStruct((len(left), len(right), 1, 2, width), jnp.float32),
        in_specs=[vmem] * len(arrays),
        out_specs=pl.BlockSpec(memory_space=pltpu.HBM),
        scratch_shapes=[
            pltpu.VMEM((len(left), len(right), 1, 2, width), jnp.float32),
            pltpu.SemaphoreType.DMA((width // LANES,)),
        ],
        compiler_params=pltpu.CompilerParams(vmem_limit_bytes=CROSS_VMEM),
        cost_estimate=pl.CostEstimate(flops=4 << 20, bytes_accessed=2 << 20, transcendentals=0),
        name="cross",
    )(*arrays)


def product_kernel(left_count, right_count, count, *refs):
    left, right = refs[:left_count], refs[left_count : left_count + right_count]
    products = refs[-1]
    for tile in range(products.shape[1] // 2):
        at_re = slice(2 * tile * count, (2 * tile + 1) * count)
        at_im = slice((2 * tile + 1) * count, (2 * tile + 2) * count)
        rights = [
            (ref[at_re, :].astype(jnp.float32), ref[at_im, :].astype(jnp.float32)) for ref in right
        ]
        for i, ref in enumerate(left):
            left_re = ref[at_re, :].astype(jnp.float32)
            left_im = ref[at_im, :].astype(jnp.float32)
            for j, (right_re, right_im) in enumerate(rights):
                pair = i * right_count + j
                products[pair, 2 * tile] = left_re * right_re + left_im * right_im
                products[pair, 2 * tile + 1] = left_im * right_re - left_re * right_im


def pair_products(left, right, count, width):
    pairs = len(left) * len(right)
    vmem = pl.BlockSpec(memory_space=pltpu.VMEM)
    return pl.pallas_call(
        functools.partial(product_kernel, len(left), len(right), count),
        out_shape=jax.ShapeDtypeStruct((pairs, 2 * width // LANES, count, LANES), jnp.float32),
        in_specs=[vmem] * (len(left) + len(right)),
        out_specs=vmem,
        compiler_params=pltpu.CompilerParams(vmem_limit_bytes=CROSS_VMEM),
        cost_estimate=pl.CostEstimate(flops=4 << 20, bytes_accessed=2 << 20, transcendentals=0),
        name="pair_products",
    )(*left, *right)


def sublane_sums(values):
    row = lax.broadcasted_iota(jnp.int32, (8, LANES), 0)
    for bit in (4, 2, 1):
        low = (row & bit) == 0
        packed = []
        for q in range(bit):
            a, b = values[q], values[q + bit]
            theirs = jnp.where(low, b, a)
            down = pltpu.roll(theirs, bit, 0)
            if bit < 4:
                down = jnp.where(low, pltpu.roll(theirs, 8 - bit, 0), down)
            packed.append(jnp.where(low, a, b) + down)
        values = packed
    return values[0]


def stack_kernel(left_count, right_count, channels, energy, products, out, block, sems):
    count = products.shape[2]
    weight, scale = weights_of(energy[...], count, channels)
    up, across = places_here()
    copies = []
    for tile in range(block.shape[-1] // LANES):
        cut = slice(tile * LANES, (tile + 1) * LANES)
        for i in range(left_count):
            at = up[i]
            for first in range(0, right_count, 4):
                some = range(first, min(first + 4, right_count))
                sums = []
                for j in some:
                    for part in range(2):
                        total = jnp.zeros((8, LANES), jnp.float32)
                        for begin in range(0, count, 8):
                            here = slice(begin, begin + 8)
                            product = products[i * right_count + j, 2 * tile + part, here, :]
                            total = total + product * weight[here, :]
                        sums.append(total)
                sums = sublane_sums(sums + [sums[0]] * (8 - len(sums))) * scale
                for k, j in enumerate(some):
                    block[at, across[j], 0, :, cut] = sums[2 * k : 2 * k + 2, :]
        part = (slice(None),) * 4 + (cut,)
        copies.append(pltpu.make_async_copy(block.at[part], out.at[part], sems.at[tile]))
        copies[-1].start()
    for copy in copies:
        copy.wait()


def stack(energy, products, left_count, right_count, width, channels):
    vmem = pl.BlockSpec(memory_space=pltpu.VMEM)
    shape = (left_count, right_count, 1, 2, width)
    return pl.pallas_call(
        functools.partial(stack_kernel, left_count, right_count, channels),
        out_shape=jax.ShapeDtypeStruct(shape, jnp.float32),
        in_specs=[vmem, vmem],
        out_specs=pl.BlockSpec(memory_space=pltpu.HBM),
        scratch_shapes=[
            pltpu.VMEM(shape, jnp.float32),
            pltpu.SemaphoreType.DMA((width // LANES,)),
        ],
        compiler_params=pltpu.CompilerParams(vmem_limit_bytes=CROSS_VMEM),
        cost_estimate=pl.CostEstimate(flops=4 << 20, bytes_accessed=2 << 20, transcendentals=0),
        name="stack",
    )(energy, products)


def partners(size):
    if size & (size - 1) == 0:
        return [lambda p, k=k: p ^ k for k in range(size)]
    return [lambda p, k=k: (p - k) % size for k in range(size)]


def fetch(x, axis, size, step):
    source = partners(size)[step]
    return lax.ppermute(x, axis, [(source(p), p) for p in range(size)])


def fetch_all(x, axis, size):
    return [fetch(x, axis, size, step) for step in range(size - 1, 0, -1)][::-1]


def per_device(row_size, col_size, strain, offsets, bins):
    x_size, c_size, z_size, y_size = (lax.axis_size(a) for a in AXES)
    channels = row_size * col_size
    own = transform(strain, offsets, bins)

    column = [own] + fetch_all(own, "z", z_size)
    beside = fetch_all(own, "x", x_size)
    other = fetch_all(own, "y", y_size)
    forward = [fetch(w, "y", y_size, step) for w in column[1:] for step in range(1, y_size)]
    kept = own.astype(jnp.float32)
    other, forward, beside, column, kept = lax.optimization_barrier((other, forward, beside, column, kept))
    column_energy = [energy_of(w) for w in [kept] + column[1:] + other + forward]
    energy = functools.reduce(jnp.add, column_energy)

    energy, beside, column = lax.optimization_barrier((energy, beside, column))
    parts = []
    for i in range(x_size):
        for j in range(c_size):
            f, g = partners(x_size)[i], partners(c_size)[j]
            pairs = [
                (f(x) * c_size + g(c), x * c_size + c) for x in range(x_size) for c in range(c_size)
            ]
            if i or j:
                parts.append(lax.ppermute(energy, ("x", "c"), pairs))
    energy = functools.reduce(jnp.add, parts, energy)
    swapped = [column[0]] + beside
    right = [kept] + beside
    right = right + [fetch(w, "c", c_size, step) for step in range(1, c_size) for w in swapped]
    left = [kept] + column[1:] + other + forward
    count, width = offsets.shape[0], bins.shape[0]
    if len(left) * len(right) * count * 2 * width * 4 > PRODUCT_BYTES:
        return cross(energy, left, right, count, width, channels)
    products = pair_products(left, right, count, width)
    return stack(energy, products, len(left), len(right), width, channels)


def factors(size):
    return (size // 2, 2) if size % 2 == 0 else (size, 1)


def solution(mesh):
    row_size, col_size = mesh.shape["row"], mesh.shape["col"]
    shape = factors(row_size) + factors(col_size)
    fine = Mesh(mesh.devices.reshape(shape), AXES)
    return jax.shard_map(
        functools.partial(per_device, row_size, col_size),
        mesh=fine,
        in_specs=(P(("x", "c", "z", "y"), None), P(), P()),
        out_specs=P(("x", "c"), None, ("z", "y"), None, None),
        check_vma=False,
    )
```
